128 devices in a mesh: blk: 64 (over z, x, y), col: 2 (over core).
Axes of the slice: x: 4, y: 4, z: 4, core: 2. Of those that a mesh axis runs over, the one named last changes fastest.
Arguments:
- basis_rows: bfloat16 [65536, 4096], P('blk', 'col'), may hold values from -2 to 2
- screen: int32 [64, 4], P('blk'), may hold values from 0 to 1, as said below
Outputs:
- exchange_blocks: float32 [64, 5, 1024, 1024], P('blk', None, 'col')
The draws below stay inside these ranges and needn't reach their ends.
Inputs may be any that keep to these rules, and one draw needn't show every extreme that they name: `screen`: entries are zero where a + k + 1 >= 64; block 0 keeps all its 4 partners.
All inputs are finite; a program needn't handle non-finite values.
Results may differ from the reference program's by a relative error of at most 0.0003.
Values may be sent and summed in bfloat16 or wider, within the bound.
No kernel may reach another device: no remote copies, remote signals or barrier semaphores. Data moves between devices by JAX's collectives and lax.ppermute only.
A program may use at most 128 MiB of HBM per device.

```python
import jax
import jax.numpy as jnp
from jax import lax

BS = 1024
COLS = 4096
SPAN = 4
NBLK = 64
NBASIS = 65536


def draw_screen(key, part):
    key = jax.random.fold_in(key, 5)
    flags = jax.random.randint(key, (NBLK, SPAN), 0, 2)
    block = jnp.arange(NBLK)[:, None]
    reach = jnp.arange(SPAN)[None, :] + 1
    flags = jnp.where(block == 0, 1, flags)
    return jnp.where(block + reach < NBLK, flags, 0).astype(jnp.int32)


def shard_levels(key, extent, cuts, least, high):
    level = 1.0
    for axis_at, blocks in cuts:
        heights = jax.random.uniform(jax.random.fold_in(jax.random.fold_in(key, 6), axis_at), (blocks,), jnp.float32, least / len(cuts), high / len(cuts))
        level = level * jnp.repeat(jnp.exp(heights), extent[axis_at] // blocks).reshape((-1,) + (1,) * (len(extent) - 1 - axis_at))
    return level


def bell_draw(rng, dims, scale, most, cuts=(), held_as=jnp.bfloat16):
    drawn = scale * jax.random.normal(rng, dims, jnp.float32)
    if cuts:
        drawn = drawn * shard_levels(rng, dims, cuts, -0.22, 0.18)
    return jnp.clip(drawn, -most, most).astype(held_as)


def setup_inputs(seed: int = 0) -> dict:
    keys = jax.random.split(jax.random.key(seed), 3)
    basis_rows = bell_draw(keys[0], (NBASIS, COLS), 0.125, 2.0, ((0, 64), (1, 2)))
    screen = draw_screen(jax.random.fold_in(keys[2], 71), 0)
    return dict(basis_rows=basis_rows, screen=screen)


def reference(basis_rows, screen):
    padded = jnp.concatenate([basis_rows, jnp.zeros((SPAN * BS, COLS), basis_rows.dtype)], axis=0)
    flags = jnp.concatenate([jnp.ones((NBLK, 1), jnp.int32), screen], axis=1).astype(jnp.float32)

    def one_block(index):
        own = lax.dynamic_slice_in_dim(padded, index * BS, BS, 0)
        pieces = []
        for step in range(SPAN + 1):
            partner = lax.dynamic_slice_in_dim(padded, (index + step) * BS, BS, 0)
            pieces.append(jnp.dot(own, partner.T, preferred_element_type=jnp.float32))
        return jnp.stack(pieces, axis=0)

    blocks = lax.map(one_block, jnp.arange(NBLK, dtype=jnp.int32))
    return blocks * flags[:, :, None, None]
```

```python
import jax
import jax.numpy as jnp
from jax import lax
from jax.experimental import pallas as pl
from jax.experimental.pallas import tpu as pltpu
from jax.sharding import PartitionSpec as P

RING = 4
STRIP = 256
MIB = 1 << 20
SMALL = pl.CostEstimate(flops=1, bytes_accessed=1, transcendentals=0)
VMEM = pl.BlockSpec(memory_space=pltpu.VMEM)
SMEM = pl.BlockSpec(memory_space=pltpu.SMEM)
ANY = pl.BlockSpec(memory_space=pl.ANY)


def product(rows, partner):
    return lax.dot_general(
        rows, partner, (((1,), (1,)), ((), ())), preferred_element_type=jnp.float32
    )


def handed_products(handed, partners):
    height, counts = handed.shape[0], [p.shape[0] for p in partners]

    def kernel(handed_ref, *refs):
        *partner_refs, made_ref = refs

        @pl.loop(0, height // STRIP)
        def _(strip):
            at = pl.ds(pl.multiple_of(strip * STRIP, STRIP), STRIP)
            first = 0
            for ref, count in zip(partner_refs, counts):
                made_ref[at, first:first + count] = product(handed_ref[at, :], ref[...])
                first += count

    return pl.pallas_call(
        kernel,
        out_shape=jax.ShapeDtypeStruct((height, sum(counts)), jnp.float32),
        in_specs=[VMEM] * (1 + len(partners)),
        out_specs=VMEM,
        compiler_params=pltpu.CompilerParams(vmem_limit_bytes=20 * MIB),
        cost_estimate=SMALL,
    )(handed, *partners)


def kept_products(out, weights, kept, theirs, partners, places, shape):
    height, counts = kept.shape[0], [p.shape[0] for p in partners]

    def kernel(weights_ref, kept_ref, theirs_ref, *refs):
        refs = list(refs)
        partner_refs, refs = refs[:len(partners)], refs[len(partners):]
        if out is not None:
            refs = refs[1:]
        out_ref, made_ref, sems = refs

        copies, first = [], 0
        for index, (ref, (k, column, _), count) in enumerate(zip(partner_refs, places, counts)):
            across = pl.ds(first, count)

            @pl.loop(0, height // STRIP)
            def _(strip):
                at = pl.ds(pl.multiple_of(strip * STRIP, STRIP), STRIP)
                total = product(kept_ref[at, :], ref[...]) + theirs_ref[at, across]
                made_ref[at, across] = total * weights_ref[k]

            copy = pltpu.make_async_copy(
                made_ref.at[:, across], out_ref.at[k, :, pl.ds(column, count)], sems.at[index]
            )
            copy.start()
            copies.append(copy)
            first += count
        for copy in copies:
            copy.wait()

    first_call = out is None
    return pl.pallas_call(
        kernel,
        out_shape=jax.ShapeDtypeStruct(shape, jnp.float32),
        in_specs=[SMEM] + [VMEM] * (2 + len(partners)) + ([] if first_call else [ANY]),
        out_specs=ANY,
        scratch_shapes=[
            pltpu.VMEM((height, sum(counts)), jnp.float32),
            pltpu.SemaphoreType.DMA((len(partners),)),
        ],
        input_output_aliases={} if first_call else {3 + len(partners): 0},
        compiler_params=pltpu.CompilerParams(vmem_limit_bytes=20 * MIB),
        cost_estimate=SMALL,
    )(weights, kept, theirs, *partners, *([] if first_call else [out]))


def body(basis_rows, screen):
    blocks = lax.axis_size("blk")
    height = basis_rows.shape[0]
    half = height // 2
    column = lax.axis_index("blk") % RING
    core = lax.axis_index("col")
    weights = jnp.concatenate([jnp.ones((1,), jnp.float32), screen[0].astype(jnp.float32)])

    def below(distance):
        return [(i, (i - distance) % blocks) for i in range(blocks)]

    def around(distance):
        return [(i, i - i % RING + (i + distance) % RING) for i in range(blocks)]

    def rows(array, first, count):
        return lax.slice_in_dim(array, first, first + count, axis=0)

    q = height // 4
    phases = [
        dict(send=[("4", 0, q)], make=[(0, 0, height)]),
        dict(send=[("4", q, q), ("1", 0, q), ("3", 0, q)], make=[(4, 0, q)]),
        dict(send=[("4", 2 * q, q), ("1", q, q), ("3", q, q)], make=[(4, q, q), (1, 0, q), (3, 0, q)]),
        dict(send=[("4", 3 * q, q), ("1", 2 * q, q), ("3", 2 * q, q)], make=[(4, 2 * q, q), (1, q, q), (3, q, q)]),
        dict(send=[("1", 3 * q, q), ("3", 3 * q, q)], make=[(4, 3 * q, q), (1, 2 * q, q), (3, 2 * q, q)]),
        dict(send=[("2-", 2 * q, q), ("2+", 0, q)], make=[(1, 3 * q, q), (3, 3 * q, q)]),
        dict(send=[("2-", 3 * q, q), ("2+", q, q)], make=[(2, 2 * q, q), (2, 0, q)]),
        dict(send=[], make=[(2, 3 * q, q), (2, q, q)]),
    ]

    own = basis_rows
    kept = lax.dynamic_slice_in_dim(own, core * half, half, 0)
    handed = lax.dynamic_slice_in_dim(own, (1 - core) * half, half, 0)
    out = None
    held = {0: {(0, height): own}, 1: {}, 2: {}, 3: {}, 4: {}}
    ready = {}

    def part(k, first, count):
        for (start, size), array in held[k].items():
            if start <= first and first + count <= start + size:
                return rows(array, first - start, count)
        raise KeyError

    def operand(how, first, count):
        if how == "4":
            return part(0, first, count)
        if how == "1":
            return jnp.where(column == 0, part(4, first, count), part(0, first, count))
        if how == "3":
            return jnp.where(column == RING - 1, part(0, first, count), part(4, first, count))
        return part(1 if how == "2-" else 3, first, count)

    routes = {
        "4": (4, below(4)), "1": (1, around(-1)),
        "3": (3, around(1)), "2-": (2, below(1)), "2+": (2, below(-1)),
    }

    across = [(0, 1), (1, 0)]
    made, waiting = None, None
    for index, phase in enumerate(phases):
        last = index + 1 == len(phases)
        arrived = {}
        for how, first, count in phase["send"]:
            k, route = routes[how]
            send = ready.pop((how, first, count), None)
            if send is None:
                send = operand(how, first, count)
            arrived[k, first, count] = lax.ppermute(send, "blk", route)
        if made is not None:
            theirs = lax.ppermute(made, "col", across)
            partners = [part(*piece) for piece in waiting]
            out = kept_products(out, weights, kept, theirs, partners, waiting, (5, half, height))
        waiting = phase["make"]
        made = handed_products(handed, [part(*piece) for piece in waiting])
        if last:
            break
        for how, first, count in phases[index + 1]["send"]:
            if how == "4":
                ready[how, first, count] = operand(how, first, count)
        for (k, first, count), array in arrived.items():
            held[k][first, count] = array
        state = (held, ready, kept, handed, made, out)
        held, ready, kept, handed, made, out = lax.optimization_barrier(state)
    theirs = lax.ppermute(made, "col", across)
    partners = [part(*piece) for piece in waiting]
    out = kept_products(out, weights, kept, theirs, partners, waiting, (5, half, height))
    return out[None]


def solution(mesh):
    return jax.shard_map(
        body,
        mesh=mesh,
        in_specs=(P("blk", "col"), P("blk", None)),
        out_specs=P("blk", None, "col", None),
        check_vma=False,
    )
```

```python
import jax
import jax.numpy as jnp
from jax import lax
from jax.experimental import pallas as pl
from jax.experimental.pallas import tpu as pltpu
from jax.sharding import PartitionSpec as P

RING = 4
STRIP = 256
MIB = 1 << 20
SMALL = pl.CostEstimate(flops=1, bytes_accessed=1, transcendentals=0)
VMEM = pl.BlockSpec(memory_space=pltpu.VMEM)
SMEM = pl.BlockSpec(memory_space=pltpu.SMEM)
ANY = pl.BlockSpec(memory_space=pl.ANY)
LIMIT = pltpu.CompilerParams(vmem_limit_bytes=28 * MIB)


def product(rows, partner):
    return lax.dot_general(
        rows, partner, (((1,), (1,)), ((), ())), preferred_element_type=jnp.float32
    )


def strips(height, run):
    @pl.loop(0, height // STRIP)
    def _(strip):
        run(pl.ds(pl.multiple_of(strip * STRIP, STRIP), STRIP))


def columns(group):
    first = 0
    for k, start, count in group:
        yield (k, start, count), pl.ds(first, count)
        first += count


def width(group):
    return sum(count for _, _, count in group)


def handed_products(handed, partners, group):
    height, arrays = handed.shape[0], list({id(p): p for p, _ in partners}.values())
    which = [[p is array for array in arrays].index(True) for p, _ in partners]

    def kernel(handed_ref, *refs):
        *array_refs, made_ref = refs
        for ((_, _, count), across), (_, start), at_array in zip(columns(group), partners, which):
            def strip(at):
                partner = array_refs[at_array][start:start + count, :]
                made_ref[at, across] = product(handed_ref[at, :], partner)
            strips(height, strip)

    return pl.pallas_call(
        kernel,
        out_shape=jax.ShapeDtypeStruct((height, width(group)), jnp.float32),
        in_specs=[VMEM] * (1 + len(arrays)),
        out_specs=VMEM,
        compiler_params=LIMIT,
        cost_estimate=SMALL,
    )(handed, *arrays)


def kept_products(out, weights, kept, theirs, partners, group, shape):
    height, arrays = kept.shape[0], list({id(p): p for p, _ in partners}.values())
    which = [[p is array for array in arrays].index(True) for p, _ in partners]
    first_call = out is None

    def kernel(weights_ref, kept_ref, theirs_ref, *refs):
        array_refs, refs = refs[:len(arrays)], refs[len(arrays):]
        out_ref, made_ref, sems = refs if first_call else refs[1:]
        copies = []
        for ((k, first, count), across), (_, start), at_array in zip(columns(group), partners, which):
            def strip(at):
                partner = array_refs[at_array][start:start + count, :]
                total = product(kept_ref[at, :], partner) + theirs_ref[at, across]
                made_ref[at, across] = total * weights_ref[k]
            strips(height, strip)
            copy = pltpu.make_async_copy(
                made_ref.at[:, across],
                out_ref.at[k, :, pl.ds(first, count)],
                sems.at[len(copies)],
            )
            copy.start()
            copies.append(copy)
        for copy in copies:
            copy.wait()

    return pl.pallas_call(
        kernel,
        out_shape=jax.ShapeDtypeStruct(shape, jnp.float32),
        in_specs=[SMEM] + [VMEM] * (2 + len(arrays)) + [ANY] * (not first_call),
        out_specs=ANY,
        scratch_shapes=[
            pltpu.VMEM((height, width(group)), jnp.float32),
            pltpu.SemaphoreType.DMA((len(group),)),
        ],
        input_output_aliases={} if first_call else {3 + len(arrays): 0},
        compiler_params=LIMIT,
        cost_estimate=SMALL,
    )(weights, kept, theirs, *arrays, *([] if first_call else [out]))


def relayed_products(where, rows, partners, theirs=()):
    size, many, sums = rows[0].shape[0], len(rows) // 2, len(theirs) > 0
    counts = [p.shape[0] - start for p, start in partners]

    def kernel(where_ref, *refs):
        row_refs, refs = refs[:len(rows)], refs[len(rows):]
        partner_refs, refs = refs[:len(partners)], refs[len(partners):]
        lower, upper = row_refs[:many], row_refs[many:]

        def run(chosen):
            for index, row_ref in enumerate(chosen):
                at, first = pl.ds(index * size, size), 0
                for n, (partner_ref, (_, start)) in enumerate(zip(partner_refs, partners)):
                    made = product(row_ref[...], partner_ref[start:, :])
                    if sums:
                        refs[-1][at, pl.ds(first, counts[n])] = made + refs[n][at, :]
                    else:
                        refs[n][at, :] = made
                    first += counts[n]

        pl.when(where_ref[0] == 0)(lambda: run(lower if sums else upper))
        pl.when(where_ref[0] == 1)(lambda: run(upper if sums else lower))

    widths = [sum(counts)] if sums else counts
    operands = [*rows, *(p for p, _ in partners), *theirs]
    return pl.pallas_call(
        kernel,
        out_shape=[jax.ShapeDtypeStruct((many * size, w), jnp.float32) for w in widths],
        in_specs=[SMEM] + [VMEM] * len(operands),
        out_specs=[VMEM] * len(widths),
        compiler_params=LIMIT,
        cost_estimate=SMALL,
    )(where, *operands)


def scaled_write(out, weights, made, tile, shape):
    k, first, count = tile

    def kernel(weights_ref, summed_ref, _, out_ref, made_ref, sem):
        def strip(at):
            made_ref[at, :] = summed_ref[at, :] * weights_ref[k]

        strips(made.shape[0], strip)
        copy = pltpu.make_async_copy(made_ref, out_ref.at[k, :, pl.ds(first, count)], sem)
        copy.start()
        copy.wait()

    return pl.pallas_call(
        kernel,
        out_shape=jax.ShapeDtypeStruct(shape, jnp.float32),
        in_specs=[SMEM, VMEM, ANY],
        out_specs=ANY,
        scratch_shapes=[pltpu.VMEM(made.shape, jnp.float32), pltpu.SemaphoreType.DMA],
        input_output_aliases={2: 0},
        compiler_params=LIMIT,
        cost_estimate=SMALL,
    )(weights, made, out)


def body(basis_rows, screen):
    blocks = lax.axis_size("blk")
    height = basis_rows.shape[0]
    half, q = height // 2, height // 4
    column = lax.axis_index("blk") % RING
    core = lax.axis_index("col")
    weights = jnp.concatenate([jnp.ones((1,), jnp.float32), screen[0].astype(jnp.float32)])
    where = core.astype(jnp.int32)[None]
    shape = (5, half, height)

    def below(distance):
        return [(i, (i - distance) % blocks) for i in range(blocks)]

    def around(distance):
        return [(i, i - i % RING + (i + distance) % RING) for i in range(blocks)]

    def swap(array):
        return lax.ppermute(array, "col", [(0, 1), (1, 0)])

    s = dict(own=basis_rows, held={}, made={}, out=None)

    def fence(*arrived):
        s["held"].update(arrived)
        s.update(lax.optimization_barrier(s))

    def mine(j):
        s["held"][0, j] = lax.slice_in_dim(s["own"], j * q, (j + 1) * q, axis=0)

    def fetch4(j):
        return (4, j), lax.ppermute(s["held"][0, j], "blk", below(4))

    def fetch1(j):
        send = jnp.where(column == 0, s["held"][4, j], s["held"][0, j])
        return (1, j), lax.ppermute(send, "blk", around(-1))

    def fetch3(j):
        send = jnp.where(column == RING - 1, s["held"][0, j], s["held"][4, j])
        return (3, j), lax.ppermute(send, "blk", around(1))

    def partners(group):
        found = []
        for k, first, _ in group:
            if k == 0:
                found.append((s["own"], first))
            elif k == 2:
                found.append((s["relayed"], first))
            else:
                found.append((s["held"][k, first // q], first % q))
        return found

    def make(*groups):
        for group in groups:
            s["made"][group] = handed_products(s["handed"], partners(group), group)

    def finish(*groups):
        for group in groups:
            theirs = swap(s["made"].pop(group))
            s["out"] = kept_products(
                s["out"], weights, s["kept"], theirs, partners(group), group, shape
            )

    e = q // 2
    own1, own2 = ((0, 0, 3 * e),), ((0, 3 * e, 3 * e),)
    own3 = ((0, 6 * e, q), (4, 0, e))
    four1 = ((4, e, e), (4, q, q))
    four2 = ((4, 2 * q, q), (1, 0, e))
    mixed1 = ((1, e, e), (3, 0, q))
    mixed2 = ((1, q, q), (3, q, e))
    four3 = ((4, 3 * q, q), (3, q + e, e))
    mixed3 = ((1, 2 * q, q), (3, 2 * q, q))
    mixed4 = ((1, 3 * q, q), (3, 3 * q, q))

    mine(0)
    fence()
    mine(1)
    s["kept"] = lax.dynamic_slice_in_dim(s["own"], core * half, half, 0)
    s["handed"] = lax.dynamic_slice_in_dim(s["own"], (1 - core) * half, half, 0)
    x0, x1 = fetch4(0), fetch4(1)
    make(own1)
    fence(x0)
    mine(2)
    d0, u0, x2 = fetch1(0), fetch3(0), fetch4(2)
    finish(own1)
    make(own2)
    fence(x1)
    mine(3)
    d1, u1 = fetch1(1), fetch3(1)
    fence(d0, u0)
    x3 = fetch4(3)
    finish(own2)
    make(own3, four1)
    fence(x2)
    d2, u2 = fetch1(2), fetch3(2)
    fence(d1, u1)
    finish(own3, four1)
    make(four2, mixed1, mixed2)
    fence(x3)
    d3, u3 = fetch1(3), fetch3(3)
    fence(d2, u2)
    finish(four2, mixed1, mixed2)
    make(four3, mixed3)
    relay = q + e
    s["relay"] = jnp.concatenate([s["held"][1, 0], s["held"][1, 1][:e]])
    fence(d3, u3)

    relayed = lax.ppermute(s["relay"], "blk", below(1))
    rows = [s["held"][1, j] for j in range(4)]
    others = [(s["held"][3, 1], e), (s["held"][3, 2], 0), (s["held"][3, 3], 0)]
    theirs = [swap(array) for array in relayed_products(where, rows, others)]
    s["ahead"], = relayed_products(where, rows, others, theirs)
    make(mixed4)
    fence()

    ahead = lax.ppermute(s["ahead"], "blk", below(-1))
    finish(four3, mixed3, mixed4)
    s["relayed"] = relayed
    fence()

    group = ((2, 0, relay),)
    make(group)
    finish(group)
    out = scaled_write(s["out"], weights, ahead, (2, relay, height - relay), shape)
    return out[None]


def solution(mesh):
    return jax.shard_map(
        body,
        mesh=mesh,
        in_specs=(P("blk", "col"), P("blk", None)),
        out_specs=P("blk", None, "col", None),
        check_vma=False,
    )
```

```python
import jax
import jax.numpy as jnp
from jax import lax
from jax.experimental import pallas as pl
from jax.experimental.pallas import tpu as pltpu
from jax.sharding import PartitionSpec as P

RING = 4
PARTS = 4
STRIP = 512
MIB = 1 << 20
SMALL = pl.CostEstimate(flops=1, bytes_accessed=1, transcendentals=0)
VMEM = pl.BlockSpec(memory_space=pltpu.VMEM)
SMEM = pl.BlockSpec(memory_space=pltpu.SMEM)
ANY = pl.BlockSpec(memory_space=pl.ANY)
HBM = pl.BlockSpec(memory_space=pltpu.HBM)
LIMIT = pltpu.CompilerParams(vmem_limit_bytes=28 * MIB)


def product(rows, partner):
    return lax.dot_general(
        rows, partner, (((1,), (1,)), ((), ())), preferred_element_type=jnp.float32
    )


def strips(height, run):
    @pl.loop(0, height // STRIP)
    def _(strip):
        run(pl.ds(pl.multiple_of(strip * STRIP, STRIP), STRIP))


def take_rows(after, own, first, count):
    def kernel(_, own_ref, taken_ref, sem):
        copy = pltpu.make_async_copy(own_ref.at[pl.ds(first, count), :], taken_ref, sem)
        copy.start()
        copy.wait()

    return pl.pallas_call(
        kernel,
        out_shape=jax.ShapeDtypeStruct((count, own.shape[1]), own.dtype),
        in_specs=[SMEM, HBM],
        out_specs=VMEM,
        scratch_shapes=[pltpu.SemaphoreType.DMA],
        compiler_params=LIMIT,
        cost_estimate=SMALL,
    )(after, own)


def columns(group, half):
    e, first = half // PARTS, 0
    for k, part in group:
        count = 2 * half if part is None else 2 * e
        yield k, count, first, [0] if part is None else [part * e, half + part * e]
        first += count


def width(group, half):
    return sum(count for _, count, _, _ in columns(group, half))


def whole(refs):
    return refs[0][...] if len(refs) == 1 else jnp.concatenate([ref[...] for ref in refs], axis=0)


def deal(refs, partners):
    refs = iter(refs)
    return [[next(refs) for _ in arrays] for arrays in partners]


def handed_products(handed, partners, group, before=None, total=None):
    half, many = handed.shape[0], sum(map(len, partners))
    size = width(group, half)
    room = total or size
    offset = 0 if before is None else room - size

    def kernel(handed_ref, *refs):
        made_ref = refs[-1]
        for (_, count, first, _), tile_refs in zip(columns(group, half), deal(refs, partners)):
            def strip(at):
                across = pl.ds(offset + first, count)
                made_ref[at, across] = product(handed_ref[at, :], whole(tile_refs))
            strips(half, strip)

    return pl.pallas_call(
        kernel,
        out_shape=jax.ShapeDtypeStruct((half, room), jnp.float32),
        in_specs=[VMEM] * (1 + many) + [VMEM] * (before is not None),
        out_specs=VMEM,
        input_output_aliases={} if before is None else {1 + many: 0},
        compiler_params=LIMIT,
        cost_estimate=SMALL,
    )(handed, *sum(partners, []), *([] if before is None else [before]))


def kept_products(out, weights, kept, theirs, partners, groups):
    half, first_call = kept.shape[0], out is None
    many = sum(map(len, partners))

    def kernel(weights_ref, kept_ref, *refs):
        theirs_refs, refs = refs[:len(groups)], refs[len(groups):]
        partner_refs, refs = iter(deal(refs, partners)), refs[many:]
        out_ref, *made_refs, sems = refs if first_call else refs[1:]
        copies = []
        for group, theirs_ref, made_ref in zip(groups, theirs_refs, made_refs):
            for (k, count, first, runs), tile_refs in zip(columns(group, half), partner_refs):
                def strip(at):
                    across = pl.ds(first, count)
                    total = product(kept_ref[at, :], whole(tile_refs)) + theirs_ref[at, across]
                    made_ref[at, across] = total * weights_ref[k]
                strips(half, strip)
                for n, column in enumerate(runs):
                    run = count // len(runs)
                    copies.append(pltpu.make_async_copy(
                        made_ref.at[:, pl.ds(first + n * run, run)],
                        out_ref.at[k, :, pl.ds(column, run)],
                        sems.at[len(copies)],
                    ))
                    copies[-1].start()
        for copy in copies:
            copy.wait()

    inputs = len(groups) + many
    return pl.pallas_call(
        kernel,
        out_shape=jax.ShapeDtypeStruct((5, half, 2 * half), jnp.float32),
        in_specs=[SMEM] + [VMEM] * (1 + inputs) + [ANY] * (not first_call),
        out_specs=ANY,
        scratch_shapes=[pltpu.VMEM((half, width(group, half)), jnp.float32) for group in groups]
        + [pltpu.SemaphoreType.DMA((2 * sum(map(len, groups)),))],
        input_output_aliases={} if first_call else {2 + inputs: 0},
        compiler_params=LIMIT,
        cost_estimate=SMALL,
    )(weights, kept, *theirs, *sum(partners, []), *([] if first_call else [out]))


def relayed_products(where, rows, partners, blocks, theirs=()):
    e, sums = rows[0][0].shape[0], len(theirs) > 0
    sizes = {}
    for parts, _, *places in blocks:
        array, first, *starts = places[sums]
        height, size = sizes.get(array, (0, 0))
        sizes[array] = max(height, first + len(parts) * e), max(size, *(c + e for c in starts))

    def kernel(where_ref, *refs):
        row_refs, refs = deal(refs, rows), refs[2 * len(rows):]
        partner_refs, refs = deal(refs, partners), refs[2 * len(partners):]
        theirs_refs, made_refs = refs[:len(theirs)], refs[len(theirs):]

        def run(kept):
            for parts, partner, *places in blocks:
                taken = [row_refs[j][kept][...] for j in parts]
                made = product(jnp.concatenate(taken, axis=0), whole(partner_refs[partner]))
                for n in range(2):
                    piece = made[:, n * e:(n + 1) * e]
                    for (array, first, *starts), refs in zip(places[:1 + sums], (theirs_refs, made_refs)[1 - sums:]):
                        at = pl.ds(first, len(parts) * e), pl.ds(starts[n], e)
                        if refs is made_refs:
                            refs[array][at] = piece
                        else:
                            piece += refs[array][at]

        for core in range(2):
            pl.when(where_ref[0] == core)(lambda core=core: run(core if sums else 1 - core))

    operands = sum([*rows, *partners], []) + list(theirs)
    return pl.pallas_call(
        kernel,
        out_shape=[jax.ShapeDtypeStruct(sizes[n], jnp.float32) for n in sorted(sizes)],
        in_specs=[SMEM] + [VMEM] * len(operands),
        out_specs=[VMEM] * len(sizes),
        compiler_params=LIMIT,
        cost_estimate=SMALL,
    )(where, *operands)


def scaled_write(out, weights, made, k, regions):
    def kernel(weights_ref, summed_ref, _, out_ref, made_ref, sems):
        made_ref[...] = summed_ref[...] * weights_ref[k]
        copies = [
            pltpu.make_async_copy(
                made_ref.at[pl.ds(row, height), pl.ds(column, size)],
                out_ref.at[k, pl.ds(to_row, height), pl.ds(to_column, size)],
                sems.at[n],
            )
            for n, (row, column, height, size, to_row, to_column) in enumerate(regions)
        ]
        for copy in copies:
            copy.start()
        for copy in copies:
            copy.wait()

    return pl.pallas_call(
        kernel,
        out_shape=jax.ShapeDtypeStruct(out.shape, jnp.float32),
        in_specs=[SMEM, VMEM, ANY],
        out_specs=ANY,
        scratch_shapes=[
            pltpu.VMEM(made.shape, jnp.float32), pltpu.SemaphoreType.DMA((len(regions),))
        ],
        input_output_aliases={2: 0},
        compiler_params=LIMIT,
        cost_estimate=SMALL,
    )(weights, made, out)


def body(basis_rows, screen):
    blocks = lax.axis_size("blk")
    half = basis_rows.shape[0] // 2
    e = half // PARTS
    column = lax.axis_index("blk") % RING
    core = lax.axis_index("col")
    weights = jnp.concatenate([jnp.ones((1,), jnp.float32), screen[0].astype(jnp.float32)])

    def below(distance):
        return [(i, (i - distance) % blocks) for i in range(blocks)]

    def around(distance):
        return [(i, i - i % RING + (i + distance) % RING) for i in range(blocks)]

    def swap(array):
        return lax.ppermute(array, "col", [(0, 1), (1, 0)])

    s = dict(where=core.astype(jnp.int32)[None], held={}, made={}, out=None)

    def fence(*arrived):
        s["held"].update(arrived)
        s.update(lax.optimization_barrier(s))

    def mine(p):
        first = p % 2 * half + p // 2 * e
        s["held"][0, p] = take_rows(s["where"], basis_rows, first, e)

    def fetch4(p):
        return (4, p), lax.ppermute(s["held"][0, p], "blk", below(4))

    def fetch1(p):
        send = jnp.where(column == 0, s["held"][4, p], s["held"][0, p])
        return (1, p), lax.ppermute(send, "blk", around(-1))

    def fetch3(p):
        send = jnp.where(column == RING - 1, s["held"][0, p], s["held"][4, p])
        return (3, p), lax.ppermute(send, "blk", around(1))

    def part(k, j):
        if j is None:
            return [basis_rows]
        return [s["relayed"]] if k == 2 else [s["held"][k, 2 * j], s["held"][k, 2 * j + 1]]

    def partners(*groups):
        return [part(k, j) for group in groups for k, j in group]

    def make(group, new=(), total=None):
        s["made"][group] = handed_products(
            s["handed"], partners(new or group), new or group, s["made"].get(group), total
        )

    def finish(*groups):
        theirs = [swap(s["made"].pop(group)) for group in groups]
        s["out"] = kept_products(s["out"], weights, s["kept"], theirs, partners(*groups), groups)

    own, ones = ((0, None),), ((4, 0), (4, 1), (1, 0), (3, 0))
    twos, threes = ((4, 2), (1, 1), (3, 1)), ((4, 3), (1, 2), (3, 2))
    first, second = own + ones, twos + threes

    mine(0)
    fence()
    mine(1)
    s["kept"] = lax.dynamic_slice_in_dim(basis_rows, core * half, half, 0)
    s["handed"] = lax.dynamic_slice_in_dim(basis_rows, (1 - core) * half, half, 0)
    pieces = 2 * PARTS
    x = [fetch4(0), fetch4(1)]
    fence(x[0])
    d, u = [fetch1(0)], [fetch3(0)]
    for p in range(pieces - 1):
        if p + 2 < pieces:
            mine(p + 2)
            x.append(fetch4(p + 2))
        if p == 1:
            make(first, own, width(first, half))
        if p == 3:
            make(first, ones, width(first, half))
        if p == 5:
            make(second, twos, width(second, half))
        fence(x[p + 1])
        d.append(fetch1(p + 1))
        u.append(fetch3(p + 1))
        fence(d[p], u[p])

    make(second, threes, width(second, half))
    some = (0, 1, 2)
    early = [(some, n, (n, 0, 0, e), (0, 0, n * e, (2 + n) * e)) for n in range(2)]
    late = [((3,), n) + 2 * ((0, 0, n * e, (3 + n) * e),) for n in range(3)]
    late += [((j,), 2) + 2 * ((0, e, 2 * j * e, (2 * j + 1) * e),) for j in some]

    def ahead(blocks):
        rows = [part(1, j) for j in range(1 + max(max(parts) for parts, *_ in blocks))]
        others = [part(3, j) for j in range(1 + max(n for _, n, *_ in blocks))]
        theirs = [swap(array) for array in relayed_products(s["where"], rows, others, blocks)]
        return relayed_products(s["where"], rows, others, blocks, theirs)[0]

    s["ahead"] = ahead(early)
    fence(d[-1], u[-1])

    first_sums = lax.ppermute(s["ahead"], "blk", below(-1))
    relayed = lax.ppermute(jnp.concatenate(part(1, 3)), "blk", below(1))
    last_sums = lax.ppermute(ahead(late), "blk", below(-1))
    third, fourth, fifth = ((1, 3),), ((3, 3),), ((2, 3),)
    make(third)
    make(fourth)
    finish(first)
    finish(second)
    s["sums"], s["relayed"] = first_sums, relayed
    fence()

    make(fifth)
    finish(third, fourth, fifth)
    regions = [(0, n * 2 * e, 3 * e, 2 * e, 0, n * half) for n in range(2)]
    out = scaled_write(s["out"], weights, s["sums"], 2, regions)
    regions = [(0, n * 3 * e, e, 3 * e, 3 * e, n * half) for n in range(2)]
    regions += [(e, (2 * j + n) * e, e, e, j * e, n * half + 2 * e) for j in some for n in range(2)]
    out = scaled_write(out, weights, last_sums, 2, regions)
    return out[None]


def solution(mesh):
    return jax.shard_map(
        body,
        mesh=mesh,
        in_specs=(P("blk", "col"), P("blk", None)),
        out_specs=P("blk", None, "col", None),
        check_vma=False,
    )
```

```python
import jax
import jax.numpy as jnp
from jax import lax
from jax.experimental import pallas as pl
from jax.experimental.pallas import tpu as pltpu
from jax.sharding import PartitionSpec as P

RING = 4
PARTS = 4
STRIP = 512
MIB = 1 << 20
SMALL = pl.CostEstimate(flops=1, bytes_accessed=1, transcendentals=0)
VMEM = pl.BlockSpec(memory_space=pltpu.VMEM)
SMEM = pl.BlockSpec(memory_space=pltpu.SMEM)
ANY = pl.BlockSpec(memory_space=pl.ANY)
HBM = pl.BlockSpec(memory_space=pltpu.HBM)
LIMIT = pltpu.CompilerParams(vmem_limit_bytes=12 * MIB)


def product(rows, partner):
    return lax.dot_general(
        rows, partner, (((1,), (1,)), ((), ())), preferred_element_type=jnp.float32
    )


def strips(height, run):
    @pl.loop(0, height // STRIP)
    def _(strip):
        run(pl.ds(pl.multiple_of(strip * STRIP, STRIP), STRIP))


def take_rows(after, own, first, count):
    def kernel(_, own_ref, taken_ref, sem):
        copy = pltpu.make_async_copy(own_ref.at[pl.ds(first, count), :], taken_ref, sem)
        copy.start()
        copy.wait()

    return pl.pallas_call(
        kernel,
        out_shape=jax.ShapeDtypeStruct((count, own.shape[1]), own.dtype),
        in_specs=[SMEM, HBM],
        out_specs=VMEM,
        scratch_shapes=[pltpu.SemaphoreType.DMA],
        compiler_params=LIMIT,
        cost_estimate=SMALL,
    )(after, own)


def columns(group, half):
    e, first = half // PARTS, 0
    for k, part in group:
        count = 2 * half if part is None else 2 * e
        yield k, count, first, [0] if part is None else [part * e, half + part * e]
        first += count


def width(group, half):
    return sum(count for _, count, _, _ in columns(group, half))


def whole(refs):
    return refs[0][...] if len(refs) == 1 else jnp.concatenate([ref[...] for ref in refs], axis=0)


def deal(refs, partners):
    refs = iter(refs)
    return [[next(refs) for _ in arrays] for arrays in partners]


def handed_products(handed, partners, group, before=None, total=None):
    half, many = handed.shape[0], sum(map(len, partners))
    size = width(group, half)
    room = total or size
    offset = 0 if before is None else room - size

    def kernel(handed_ref, *refs):
        made_ref = refs[-1]
        for (_, count, first, _), tile_refs in zip(columns(group, half), deal(refs, partners)):
            def strip(at):
                across = pl.ds(offset + first, count)
                made_ref[at, across] = product(handed_ref[at, :], whole(tile_refs))
            strips(half, strip)

    return pl.pallas_call(
        kernel,
        out_shape=jax.ShapeDtypeStruct((half, room), jnp.float32),
        in_specs=[VMEM] * (1 + many) + [VMEM] * (before is not None),
        out_specs=VMEM,
        input_output_aliases={} if before is None else {1 + many: 0},
        compiler_params=LIMIT,
        cost_estimate=SMALL,
    )(handed, *sum(partners, []), *([] if before is None else [before]))


def kept_products(out, weights, kept, theirs, partners, groups):
    half, first_call = kept.shape[0], out is None
    many = sum(map(len, partners))

    def kernel(weights_ref, kept_ref, *refs):
        theirs_refs, refs = refs[:len(groups)], refs[len(groups):]
        partner_refs, refs = iter(deal(refs, partners)), refs[many:]
        out_ref, *made_refs, sems = refs if first_call else refs[1:]
        copies = []
        for group, theirs_ref, made_ref in zip(groups, theirs_refs, made_refs):
            for (k, count, first, runs), tile_refs in zip(columns(group, half), partner_refs):
                def strip(at):
                    across = pl.ds(first, count)
                    total = product(kept_ref[at, :], whole(tile_refs)) + theirs_ref[at, across]
                    made_ref[at, across] = total * weights_ref[k]
                strips(half, strip)
                for n, column in enumerate(runs):
                    run = count // len(runs)
                    copies.append(pltpu.make_async_copy(
                        made_ref.at[:, pl.ds(first + n * run, run)],
                        out_ref.at[k, :, pl.ds(column, run)],
                        sems.at[len(copies)],
                    ))
                    copies[-1].start()
        for copy in copies:
            copy.wait()

    inputs = len(groups) + many
    return pl.pallas_call(
        kernel,
        out_shape=jax.ShapeDtypeStruct((5, half, 2 * half), jnp.float32),
        in_specs=[SMEM] + [VMEM] * (1 + inputs) + [ANY] * (not first_call),
        out_specs=ANY,
        scratch_shapes=[pltpu.VMEM((half, width(group, half)), jnp.float32) for group in groups]
        + [pltpu.SemaphoreType.DMA((2 * sum(map(len, groups)),))],
        input_output_aliases={} if first_call else {2 + inputs: 0},
        compiler_params=LIMIT,
        cost_estimate=SMALL,
    )(weights, kept, *theirs, *sum(partners, []), *([] if first_call else [out]))


def relayed_products(where, rows, partners, blocks, theirs=()):
    e, sums = rows[0][0].shape[0], len(theirs) > 0
    sizes = {}
    for parts, _, *places in blocks:
        array, first, *starts = places[sums]
        height, size = sizes.get(array, (0, 0))
        sizes[array] = max(height, first + len(parts) * e), max(size, *(c + e for c in starts))

    def kernel(where_ref, *refs):
        row_refs, refs = deal(refs, rows), refs[2 * len(rows):]
        partner_refs, refs = deal(refs, partners), refs[2 * len(partners):]
        theirs_refs, made_refs = refs[:len(theirs)], refs[len(theirs):]

        def run(kept):
            for parts, partner, *places in blocks:
                taken = [row_refs[j][kept][...] for j in parts]
                made = product(jnp.concatenate(taken, axis=0), whole(partner_refs[partner]))
                for n in range(2):
                    piece = made[:, n * e:(n + 1) * e]
                    for (array, first, *starts), refs in zip(places[:1 + sums], (theirs_refs, made_refs)[1 - sums:]):
                        at = pl.ds(first, len(parts) * e), pl.ds(starts[n], e)
                        if refs is made_refs:
                            refs[array][at] = piece
                        else:
                            piece += refs[array][at]

        for core in range(2):
            pl.when(where_ref[0] == core)(lambda core=core: run(core if sums else 1 - core))

    operands = sum([*rows, *partners], []) + list(theirs)
    return pl.pallas_call(
        kernel,
        out_shape=[jax.ShapeDtypeStruct(sizes[n], jnp.float32) for n in sorted(sizes)],
        in_specs=[SMEM] + [VMEM] * len(operands),
        out_specs=[VMEM] * len(sizes),
        compiler_params=LIMIT,
        cost_estimate=SMALL,
    )(where, *operands)


def scaled_write(out, weights, made, k, regions):
    def kernel(weights_ref, summed_ref, _, out_ref, made_ref, sems):
        made_ref[...] = summed_ref[...] * weights_ref[k]
        copies = [
            pltpu.make_async_copy(
                made_ref.at[pl.ds(row, height), pl.ds(column, size)],
                out_ref.at[k, pl.ds(to_row, height), pl.ds(to_column, size)],
                sems.at[n],
            )
            for n, (row, column, height, size, to_row, to_column) in enumerate(regions)
        ]
        for copy in copies:
            copy.start()
        for copy in copies:
            copy.wait()

    return pl.pallas_call(
        kernel,
        out_shape=jax.ShapeDtypeStruct(out.shape, jnp.float32),
        in_specs=[SMEM, VMEM, ANY],
        out_specs=ANY,
        scratch_shapes=[
            pltpu.VMEM(made.shape, jnp.float32), pltpu.SemaphoreType.DMA((len(regions),))
        ],
        input_output_aliases={2: 0},
        compiler_params=LIMIT,
        cost_estimate=SMALL,
    )(weights, made, out)


def body(basis_rows, screen):
    blocks = lax.axis_size("blk")
    half = basis_rows.shape[0] // 2
    e = half // PARTS
    column = lax.axis_index("blk") % RING
    core = lax.axis_index("col")
    weights = jnp.concatenate([jnp.ones((1,), jnp.float32), screen[0].astype(jnp.float32)])

    def below(distance):
        return [(i, (i - distance) % blocks) for i in range(blocks)]

    def around(distance):
        return [(i, i - i % RING + (i + distance) % RING) for i in range(blocks)]

    def swap(array):
        return lax.ppermute(array, "col", [(0, 1), (1, 0)])

    s = dict(where=core.astype(jnp.int32)[None], held={}, made={}, out=None)

    def fence(*arrived):
        s["held"].update(arrived)
        s.update(lax.optimization_barrier(s))

    def mine(p):
        first = p % 2 * half + p // 2 * e
        s["held"][0, p] = take_rows(s["where"], basis_rows, first, e)

    def fetch4(p):
        return (4, p), lax.ppermute(s["held"][0, p], "blk", below(4))

    def fetch1(p):
        send = jnp.where(column == 0, s["held"][4, p], s["held"][0, p])
        return (1, p), lax.ppermute(send, "blk", around(-1))

    def fetch3(p):
        send = jnp.where(column == RING - 1, s["held"][0, p], s["held"][4, p])
        return (3, p), lax.ppermute(send, "blk", around(1))

    def part(k, j):
        if j is None:
            return [basis_rows]
        return [s["relayed"]] if k == 2 else [s["held"][k, 2 * j], s["held"][k, 2 * j + 1]]

    def partners(*groups):
        return [part(k, j) for group in groups for k, j in group]

    def make(group, new=(), total=None):
        s["made"][group] = handed_products(
            s["handed"], partners(new or group), new or group, s["made"].get(group), total
        )

    def finish(*groups):
        theirs = [swap(s["made"].pop(group)) for group in groups]
        s["out"] = kept_products(s["out"], weights, s["kept"], theirs, partners(*groups), groups)

    own, ones = ((0, None),), ((4, 0), (4, 1), (1, 0), (3, 0))
    twos, threes = ((4, 2), (1, 1), (3, 1)), ((4, 3), (1, 2), (3, 2))
    first, second = own + ones, twos + threes

    mine(0)
    fence()
    mine(1)
    s["kept"] = lax.dynamic_slice_in_dim(basis_rows, core * half, half, 0)
    s["handed"] = lax.dynamic_slice_in_dim(basis_rows, (1 - core) * half, half, 0)
    pieces = 2 * PARTS
    x = [fetch4(0), fetch4(1)]
    fence(x[0])
    d, u = [fetch1(0)], [fetch3(0)]
    for p in range(pieces - 1):
        if p + 2 < pieces:
            mine(p + 2)
            x.append(fetch4(p + 2))
        if p == 1:
            make(first, own, width(first, half))
        if p == 3:
            make(first, ones, width(first, half))
        if p == 5:
            make(second, twos, width(second, half))
        fence(x[p + 1])
        d.append(fetch1(p + 1))
        u.append(fetch3(p + 1))
        fence(d[p], u[p])

    make(second, threes, width(second, half))
    some = (0, 1, 2)
    early = [(some, n, (n, 0, 0, e), (0, 0, n * e, (2 + n) * e)) for n in range(2)]
    late = [((3,), n) + 2 * ((0, 0, n * e, (3 + n) * e),) for n in range(3)]
    late += [((j,), 2) + 2 * ((0, e, 2 * j * e, (2 * j + 1) * e),) for j in some]

    def ahead(blocks):
        rows = [part(1, j) for j in range(1 + max(max(parts) for parts, *_ in blocks))]
        others = [part(3, j) for j in range(1 + max(n for _, n, *_ in blocks))]
        theirs = [swap(array) for array in relayed_products(s["where"], rows, others, blocks)]
        return relayed_products(s["where"], rows, others, blocks, theirs)[0]

    s["ahead"] = ahead(early)
    fence(d[-1], u[-1])

    first_sums = lax.ppermute(s["ahead"], "blk", below(-1))
    relayed = lax.ppermute(jnp.concatenate(part(1, 3)), "blk", below(1))
    last_sums = lax.ppermute(ahead(late), "blk", below(-1))
    third, fourth, fifth = ((1, 3),), ((3, 3),), ((2, 3),)
    make(third)
    make(fourth)
    finish(first)
    finish(second)
    s["sums"], s["relayed"] = first_sums, relayed
    fence()

    make(fifth)
    finish(third, fourth, fifth)
    regions = [(0, n * 2 * e, 3 * e, 2 * e, 0, n * half) for n in range(2)]
    out = scaled_write(s["out"], weights, s["sums"], 2, regions)
    regions = [(0, n * 3 * e, e, 3 * e, 3 * e, n * half) for n in range(2)]
    regions += [(e, (2 * j + n) * e, e, e, j * e, n * half + 2 * e) for j in some for n in range(2)]
    out = scaled_write(out, weights, last_sums, 2, regions)
    return out[None]


def solution(mesh):
    return jax.shard_map(
        body,
        mesh=mesh,
        in_specs=(P("blk", "col"), P("blk", None)),
        out_specs=P("blk", None, "col", None),
        check_vma=False,
    )
```

```python
import jax
import jax.numpy as jnp
from jax import lax
from jax.experimental import pallas as pl
from jax.experimental.pallas import tpu as pltpu
from jax.sharding import PartitionSpec as P

RING = 4
PARTS = 4
STRIP = 512
MIB = 1 << 20
SMALL = pl.CostEstimate(flops=1, bytes_accessed=1, transcendentals=0)
VMEM = pl.BlockSpec(memory_space=pltpu.VMEM)
SMEM = pl.BlockSpec(memory_space=pltpu.SMEM)
ANY = pl.BlockSpec(memory_space=pl.ANY)
HBM = pl.BlockSpec(memory_space=pltpu.HBM)
LIMIT = pltpu.CompilerParams(vmem_limit_bytes=12 * MIB)


def product(rows, partner):
    return lax.dot_general(
        rows, partner, (((1,), (1,)), ((), ())), preferred_element_type=jnp.float32
    )


def strips(height, run):
    @pl.loop(0, height // STRIP)
    def _(strip):
        run(pl.ds(pl.multiple_of(strip * STRIP, STRIP), STRIP))


def take_rows(after, own, first, count):
    def kernel(_, own_ref, taken_ref, sem):
        copy = pltpu.make_async_copy(own_ref.at[pl.ds(first, count), :], taken_ref, sem)
        copy.start()
        copy.wait()

    return pl.pallas_call(
        kernel,
        out_shape=jax.ShapeDtypeStruct((count, own.shape[1]), own.dtype),
        in_specs=[SMEM, HBM],
        out_specs=VMEM,
        scratch_shapes=[pltpu.SemaphoreType.DMA],
        compiler_params=LIMIT,
        cost_estimate=SMALL,
    )(after, own)


def columns(group, half):
    e, first = half // PARTS, 0
    for k, part in group:
        count = 2 * half if part is None else 2 * e
        yield k, count, first, [0] if part is None else [part * e, half + part * e]
        first += count


def width(group, half):
    return sum(count for _, count, _, _ in columns(group, half))


def spans(refs, count, e, run):
    if len(refs) > 1 or count == 2 * e:
        run(0, count, lambda: whole(refs))
        return

    @pl.loop(0, count // (2 * e))
    def _(index):
        at = pl.multiple_of(index * 2 * e, 2 * e)
        run(at, 2 * e, lambda: refs[0][pl.ds(at, 2 * e), :])


def whole(refs):
    return refs[0][...] if len(refs) == 1 else jnp.concatenate([ref[...] for ref in refs], axis=0)


def deal(refs, partners):
    refs = iter(refs)
    return [[next(refs) for _ in arrays] for arrays in partners]


def handed_products(handed, partners, group, before=None, total=None):
    half, many = handed.shape[0], sum(map(len, partners))
    size = width(group, half)
    room = total or size
    offset = 0 if before is None else room - size

    def kernel(handed_ref, *refs):
        made_ref = refs[-1]
        for (_, count, first, _), tile_refs in zip(columns(group, half), deal(refs, partners)):
            def span(column, columns, partner):
                def strip(at):
                    across = pl.ds(offset + first + column, columns)
                    made_ref[at, across] = product(handed_ref[at, :], partner())
                strips(half, strip)

            spans(tile_refs, count, half // PARTS, span)

    return pl.pallas_call(
        kernel,
        out_shape=jax.ShapeDtypeStruct((half, room), jnp.float32),
        in_specs=[VMEM] * (1 + many) + [VMEM] * (before is not None),
        out_specs=VMEM,
        input_output_aliases={} if before is None else {1 + many: 0},
        compiler_params=LIMIT,
        cost_estimate=SMALL,
    )(handed, *sum(partners, []), *([] if before is None else [before]))


def kept_products(out, weights, kept, theirs, partners, groups):
    half, first_call = kept.shape[0], out is None
    many = sum(map(len, partners))

    def kernel(weights_ref, kept_ref, *refs):
        theirs_refs, refs = refs[:len(groups)], refs[len(groups):]
        partner_refs, refs = iter(deal(refs, partners)), refs[many:]
        out_ref, *made_refs, sems = refs if first_call else refs[1:]
        copies = []
        for group, theirs_ref, made_ref in zip(groups, theirs_refs, made_refs):
            for (k, count, first, runs), tile_refs in zip(columns(group, half), partner_refs):
                def span(column, columns, partner):
                    def strip(at):
                        across = pl.ds(first + column, columns)
                        total = product(kept_ref[at, :], partner()) + theirs_ref[at, across]
                        made_ref[at, across] = total * weights_ref[k]
                    strips(half, strip)

                spans(tile_refs, count, half // PARTS, span)
                for n, column in enumerate(runs):
                    run = count // len(runs)
                    copies.append(pltpu.make_async_copy(
                        made_ref.at[:, pl.ds(first + n * run, run)],
                        out_ref.at[k, :, pl.ds(column, run)],
                        sems.at[len(copies)],
                    ))
                    copies[-1].start()
        for copy in copies:
            copy.wait()

    inputs = len(groups) + many
    return pl.pallas_call(
        kernel,
        out_shape=jax.ShapeDtypeStruct((5, half, 2 * half), jnp.float32),
        in_specs=[SMEM] + [VMEM] * (1 + inputs) + [ANY] * (not first_call),
        out_specs=ANY,
        scratch_shapes=[pltpu.VMEM((half, width(group, half)), jnp.float32) for group in groups]
        + [pltpu.SemaphoreType.DMA((2 * sum(map(len, groups)),))],
        input_output_aliases={} if first_call else {2 + inputs: 0},
        compiler_params=LIMIT,
        cost_estimate=SMALL,
    )(weights, kept, *theirs, *sum(partners, []), *([] if first_call else [out]))


def relayed_products(where, rows, partners, blocks, theirs=()):
    e, sums = rows[0][0].shape[0], len(theirs) > 0
    used = sorted({j for parts, *_ in blocks for j in parts})
    sizes = {}
    for parts, _, *places in blocks:
        array, first, *starts = places[sums]
        height, size = sizes.get(array, (0, 0))
        sizes[array] = max(height, first + len(parts) * e), max(size, *(c + e for c in starts))

    def kernel(where_ref, *refs):
        row_refs, refs = deal(refs, rows), refs[2 * len(rows):]
        partner_refs, refs = deal(refs, partners), refs[2 * len(partners):]
        theirs_refs, (*made_refs, taken_ref) = refs[:len(theirs)], refs[len(theirs):]

        def take(kept):
            for n, j in enumerate(used):
                taken_ref[pl.ds(n * e, e), :] = row_refs[j][kept][...]

        for core in range(2):
            pl.when(where_ref[0] == core)(lambda core=core: take(core if sums else 1 - core))

        for parts, partner, *places in blocks:
            taken = taken_ref[pl.ds(used.index(parts[0]) * e, len(parts) * e), :]
            made = product(taken, whole(partner_refs[partner]))
            for n in range(2):
                piece = made[:, n * e:(n + 1) * e]
                if sums:
                    array, first, *starts = places[0]
                    piece += theirs_refs[array][pl.ds(first, len(parts) * e), pl.ds(starts[n], e)]
                array, first, *starts = places[sums]
                made_refs[array][pl.ds(first, len(parts) * e), pl.ds(starts[n], e)] = piece

    operands = sum([*rows, *partners], []) + list(theirs)
    return pl.pallas_call(
        kernel,
        out_shape=[jax.ShapeDtypeStruct(sizes[n], jnp.float32) for n in sorted(sizes)],
        in_specs=[SMEM] + [VMEM] * len(operands),
        out_specs=[VMEM] * len(sizes),
        scratch_shapes=[pltpu.VMEM((len(used) * e, rows[0][0].shape[1]), rows[0][0].dtype)],
        compiler_params=LIMIT,
        cost_estimate=SMALL,
    )(where, *operands)


def scaled_write(out, weights, made, k, regions):
    def kernel(weights_ref, summed_ref, _, out_ref, made_ref, sems):
        made_ref[...] = summed_ref[...] * weights_ref[k]
        copies = [
            pltpu.make_async_copy(
                made_ref.at[pl.ds(row, height), pl.ds(column, size)],
                out_ref.at[k, pl.ds(to_row, height), pl.ds(to_column, size)],
                sems.at[n],
            )
            for n, (row, column, height, size, to_row, to_column) in enumerate(regions)
        ]
        for copy in copies:
            copy.start()
        for copy in copies:
            copy.wait()

    return pl.pallas_call(
        kernel,
        out_shape=jax.ShapeDtypeStruct(out.shape, jnp.float32),
        in_specs=[SMEM, VMEM, ANY],
        out_specs=ANY,
        scratch_shapes=[
            pltpu.VMEM(made.shape, jnp.float32), pltpu.SemaphoreType.DMA((len(regions),))
        ],
        input_output_aliases={2: 0},
        compiler_params=LIMIT,
        cost_estimate=SMALL,
    )(weights, made, out)


def body(basis_rows, screen):
    blocks = lax.axis_size("blk")
    half = basis_rows.shape[0] // 2
    e = half // PARTS
    column = lax.axis_index("blk") % RING
    core = lax.axis_index("col")
    weights = jnp.concatenate([jnp.ones((1,), jnp.float32), screen[0].astype(jnp.float32)])

    def below(distance):
        return [(i, (i - distance) % blocks) for i in range(blocks)]

    def around(distance):
        return [(i, i - i % RING + (i + distance) % RING) for i in range(blocks)]

    def swap(array):
        return lax.ppermute(array, "col", [(0, 1), (1, 0)])

    s = dict(where=core.astype(jnp.int32)[None], held={}, made={}, out=None)

    def fence(*arrived):
        s["held"].update(arrived)
        s.update(lax.optimization_barrier(s))

    def mine(p):
        first = p % 2 * half + p // 2 * e
        s["held"][0, p] = take_rows(s["where"], basis_rows, first, e)

    def fetch4(p):
        return (4, p), lax.ppermute(s["held"][0, p], "blk", below(4))

    def fetch1(p):
        send = jnp.where(column == 0, s["held"][4, p], s["held"][0, p])
        return (1, p), lax.ppermute(send, "blk", around(-1))

    def fetch3(p):
        send = jnp.where(column == RING - 1, s["held"][0, p], s["held"][4, p])
        return (3, p), lax.ppermute(send, "blk", around(1))

    def part(k, j):
        if j is None:
            return [basis_rows]
        return [s["relayed"]] if k == 2 else [s["held"][k, 2 * j], s["held"][k, 2 * j + 1]]

    def partners(*groups):
        return [part(k, j) for group in groups for k, j in group]

    def make(group, new=(), total=None):
        s["made"][group] = handed_products(
            s["handed"], partners(new or group), new or group, s["made"].get(group), total
        )

    def finish(*groups):
        theirs = [swap(s["made"].pop(group)) for group in groups]
        s["out"] = kept_products(s["out"], weights, s["kept"], theirs, partners(*groups), groups)

    own, ones = ((0, None),), ((4, 0), (4, 1), (1, 0), (3, 0))
    twos, threes = ((4, 2), (1, 1), (3, 1)), ((4, 3), (1, 2), (3, 2))
    first, second = own + ones, twos + threes

    mine(0)
    fence()
    mine(1)
    s["kept"] = lax.dynamic_slice_in_dim(basis_rows, core * half, half, 0)
    s["handed"] = lax.dynamic_slice_in_dim(basis_rows, (1 - core) * half, half, 0)
    pieces = 2 * PARTS
    x = [fetch4(0), fetch4(1)]
    fence(x[0])
    d, u = [fetch1(0)], [fetch3(0)]
    for p in range(pieces - 1):
        if p + 2 < pieces:
            mine(p + 2)
            x.append(fetch4(p + 2))
        if p == 1:
            make(first, own, width(first, half))
        if p == 3:
            make(first, ones, width(first, half))
        if p == 5:
            make(second, twos, width(second, half))
        fence(x[p + 1])
        d.append(fetch1(p + 1))
        u.append(fetch3(p + 1))
        fence(d[p], u[p])

    make(second, threes, width(second, half))
    some = (0, 1, 2)
    early = [(some, n, (n, 0, 0, e), (0, 0, n * e, (2 + n) * e)) for n in range(2)]
    late = [((3,), n) + 2 * ((0, 0, n * e, (3 + n) * e),) for n in range(3)]
    late += [((j,), 2) + 2 * ((0, e, 2 * j * e, (2 * j + 1) * e),) for j in some]

    def ahead(blocks):
        rows = [part(1, j) for j in range(1 + max(max(parts) for parts, *_ in blocks))]
        others = [part(3, j) for j in range(1 + max(n for _, n, *_ in blocks))]
        theirs = [swap(array) for array in relayed_products(s["where"], rows, others, blocks)]
        return relayed_products(s["where"], rows, others, blocks, theirs)[0]

    s["ahead"] = ahead(early)
    fence(d[-1], u[-1])

    first_sums = lax.ppermute(s["ahead"], "blk", below(-1))
    relayed = lax.ppermute(jnp.concatenate(part(1, 3)), "blk", below(1))
    last_sums = lax.ppermute(ahead(late), "blk", below(-1))
    third, fourth, fifth = ((1, 3),), ((3, 3),), ((2, 3),)
    make(third)
    make(fourth)
    finish(first)
    finish(second)
    s["sums"], s["relayed"] = first_sums, relayed
    fence()

    make(fifth)
    finish(third, fourth, fifth)
    regions = [(0, n * 2 * e, 3 * e, 2 * e, 0, n * half) for n in range(2)]
    out = scaled_write(s["out"], weights, s["sums"], 2, regions)
    regions = [(0, n * 3 * e, e, 3 * e, 3 * e, n * half) for n in range(2)]
    regions += [(e, (2 * j + n) * e, e, e, j * e, n * half + 2 * e) for j in some for n in range(2)]
    out = scaled_write(out, weights, last_sums, 2, regions)
    return out[None]


def solution(mesh):
    return jax.shard_map(
        body,
        mesh=mesh,
        in_specs=(P("blk", "col"), P("blk", None)),
        out_specs=P("blk", None, "col", None),
        check_vma=False,
    )
```

```python
import jax
import jax.numpy as jnp
from jax import lax
from jax.experimental import pallas as pl
from jax.experimental.pallas import tpu as pltpu
from jax.sharding import PartitionSpec as P

RING = 4
PARTS = 4
STRIP = 512
MIB = 1 << 20
SMALL = pl.CostEstimate(flops=1, bytes_accessed=1, transcendentals=0)
VMEM = pl.BlockSpec(memory_space=pltpu.VMEM)
SMEM = pl.BlockSpec(memory_space=pltpu.SMEM)
ANY = pl.BlockSpec(memory_space=pl.ANY)
HBM = pl.BlockSpec(memory_space=pltpu.HBM)
LIMIT = pltpu.CompilerParams(vmem_limit_bytes=12 * MIB)


def product(rows, partner):
    return lax.dot_general(
        rows, partner, (((1,), (1,)), ((), ())), preferred_element_type=jnp.float32
    )


def strips(height, run):
    @pl.loop(0, height // STRIP)
    def _(strip):
        run(pl.ds(pl.multiple_of(strip * STRIP, STRIP), STRIP))


def take_rows(after, own, first, count):
    def kernel(_, own_ref, taken_ref, sem):
        copy = pltpu.make_async_copy(own_ref.at[pl.ds(first, count), :], taken_ref, sem)
        copy.start()
        copy.wait()

    return pl.pallas_call(
        kernel,
        out_shape=jax.ShapeDtypeStruct((count, own.shape[1]), own.dtype),
        in_specs=[SMEM, HBM],
        out_specs=VMEM,
        scratch_shapes=[pltpu.SemaphoreType.DMA],
        compiler_params=LIMIT,
        cost_estimate=SMALL,
    )(after, own)


def columns(group, half):
    e, first = half // PARTS, 0
    for k, part in group:
        count = 2 * half if part is None else 2 * e
        yield k, count, first, [0] if part is None else [part * e, half + part * e]
        first += count


def width(group, half):
    return sum(count for _, count, _, _ in columns(group, half))


def spans(refs, count, e, run):
    if len(refs) > 1 or count == 2 * e:
        run(0, count, lambda: whole(refs))
        return

    @pl.loop(0, count // (2 * e))
    def _(index):
        at = pl.multiple_of(index * 2 * e, 2 * e)
        run(at, 2 * e, lambda: refs[0][pl.ds(at, 2 * e), :])


def whole(refs):
    return refs[0][...] if len(refs) == 1 else jnp.concatenate([ref[...] for ref in refs], axis=0)


def deal(refs, partners):
    refs = iter(refs)
    return [[next(refs) for _ in arrays] for arrays in partners]


def handed_products(handed, partners, group, before=None, room=None, offset=0):
    half, many = handed.shape[0], sum(map(len, partners))
    room = room or width(group, half)

    def kernel(handed_ref, *refs):
        made_ref = refs[-1]
        for (_, count, first, _), tile_refs in zip(columns(group, half), deal(refs, partners)):
            def span(column, columns, partner):
                def strip(at):
                    across = pl.ds(offset + first + column, columns)
                    made_ref[at, across] = product(handed_ref[at, :], partner())
                strips(half, strip)

            spans(tile_refs, count, half // PARTS, span)

    return pl.pallas_call(
        kernel,
        out_shape=jax.ShapeDtypeStruct((half, room), jnp.float32),
        in_specs=[VMEM] * (1 + many) + [VMEM] * (before is not None),
        out_specs=VMEM,
        input_output_aliases={} if before is None else {1 + many: 0},
        compiler_params=LIMIT,
        cost_estimate=SMALL,
    )(handed, *sum(partners, []), *([] if before is None else [before]))


def kept_products(out, weights, kept, theirs, partners, groups, offset=0):
    half, first_call = kept.shape[0], out is None
    many = sum(map(len, partners))

    def kernel(weights_ref, kept_ref, *refs):
        theirs_refs, refs = refs[:len(groups)], refs[len(groups):]
        partner_refs, refs = iter(deal(refs, partners)), refs[many:]
        out_ref, *made_refs, sems = refs if first_call else refs[1:]
        copies = []
        for group, theirs_ref, made_ref in zip(groups, theirs_refs, made_refs):
            for (k, count, first, runs), tile_refs in zip(columns(group, half), partner_refs):
                def span(column, columns, partner):
                    def strip(at):
                        across = pl.ds(first + column, columns)
                        there = pl.ds(offset + first + column, columns)
                        total = product(kept_ref[at, :], partner()) + theirs_ref[at, there]
                        made_ref[at, across] = total * weights_ref[k]
                    strips(half, strip)

                spans(tile_refs, count, half // PARTS, span)
                for n, column in enumerate(runs):
                    run = count // len(runs)
                    copies.append(pltpu.make_async_copy(
                        made_ref.at[:, pl.ds(first + n * run, run)],
                        out_ref.at[k, :, pl.ds(column, run)],
                        sems.at[len(copies)],
                    ))
                    copies[-1].start()
        for copy in copies:
            copy.wait()

    inputs = len(groups) + many
    return pl.pallas_call(
        kernel,
        out_shape=jax.ShapeDtypeStruct((5, half, 2 * half), jnp.float32),
        in_specs=[SMEM] + [VMEM] * (1 + inputs) + [ANY] * (not first_call),
        out_specs=ANY,
        scratch_shapes=[pltpu.VMEM((half, width(group, half)), jnp.float32) for group in groups]
        + [pltpu.SemaphoreType.DMA((2 * sum(map(len, groups)),))],
        input_output_aliases={} if first_call else {2 + inputs: 0},
        compiler_params=LIMIT,
        cost_estimate=SMALL,
    )(weights, kept, *theirs, *sum(partners, []), *([] if first_call else [out]))


def relayed_products(where, rows, partners, blocks, theirs=()):
    e, sums = rows[0][0].shape[0], len(theirs) > 0
    used = sorted({j for parts, *_ in blocks for j in parts})
    sizes = {}
    for parts, _, *places in blocks:
        array, first, *starts = places[sums]
        height, size = sizes.get(array, (0, 0))
        sizes[array] = max(height, first + len(parts) * e), max(size, *(c + e for c in starts))

    def kernel(where_ref, *refs):
        row_refs, refs = deal(refs, rows), refs[2 * len(rows):]
        partner_refs, refs = deal(refs, partners), refs[2 * len(partners):]
        theirs_refs, (*made_refs, taken_ref) = refs[:len(theirs)], refs[len(theirs):]

        def take(kept):
            for n, j in enumerate(used):
                taken_ref[pl.ds(n * e, e), :] = row_refs[j][kept][...]

        for core in range(2):
            pl.when(where_ref[0] == core)(lambda core=core: take(core if sums else 1 - core))

        for parts, partner, *places in blocks:
            taken = taken_ref[pl.ds(used.index(parts[0]) * e, len(parts) * e), :]
            made = product(taken, whole(partner_refs[partner]))
            for n in range(2):
                piece = made[:, n * e:(n + 1) * e]
                if sums:
                    array, first, *starts = places[0]
                    piece += theirs_refs[array][pl.ds(first, len(parts) * e), pl.ds(starts[n], e)]
                array, first, *starts = places[sums]
                made_refs[array][pl.ds(first, len(parts) * e), pl.ds(starts[n], e)] = piece

    operands = sum([*rows, *partners], []) + list(theirs)
    return pl.pallas_call(
        kernel,
        out_shape=[jax.ShapeDtypeStruct(sizes[n], jnp.float32) for n in sorted(sizes)],
        in_specs=[SMEM] + [VMEM] * len(operands),
        out_specs=[VMEM] * len(sizes),
        scratch_shapes=[pltpu.VMEM((len(used) * e, rows[0][0].shape[1]), rows[0][0].dtype)],
        compiler_params=LIMIT,
        cost_estimate=SMALL,
    )(where, *operands)


def scaled_write(out, weights, made, k, regions):
    def kernel(weights_ref, summed_ref, _, out_ref, made_ref, sems):
        made_ref[...] = summed_ref[...] * weights_ref[k]
        copies = [
            pltpu.make_async_copy(
                made_ref.at[pl.ds(row, height), pl.ds(column, size)],
                out_ref.at[k, pl.ds(to_row, height), pl.ds(to_column, size)],
                sems.at[n],
            )
            for n, (row, column, height, size, to_row, to_column) in enumerate(regions)
        ]
        for copy in copies:
            copy.start()
        for copy in copies:
            copy.wait()

    return pl.pallas_call(
        kernel,
        out_shape=jax.ShapeDtypeStruct(out.shape, jnp.float32),
        in_specs=[SMEM, VMEM, ANY],
        out_specs=ANY,
        scratch_shapes=[
            pltpu.VMEM(made.shape, jnp.float32), pltpu.SemaphoreType.DMA((len(regions),))
        ],
        input_output_aliases={2: 0},
        compiler_params=LIMIT,
        cost_estimate=SMALL,
    )(weights, made, out)


def body(basis_rows, screen):
    blocks = lax.axis_size("blk")
    half = basis_rows.shape[0] // 2
    e = half // PARTS
    column = lax.axis_index("blk") % RING
    core = lax.axis_index("col")
    weights = jnp.concatenate([jnp.ones((1,), jnp.float32), screen[0].astype(jnp.float32)])

    def below(distance):
        return [(i, (i - distance) % blocks) for i in range(blocks)]

    def around(distance):
        return [(i, i - i % RING + (i + distance) % RING) for i in range(blocks)]

    def swap(array):
        return lax.ppermute(array, "col", [(0, 1), (1, 0)])

    s = dict(where=core.astype(jnp.int32)[None], held={}, made={}, out=None)

    def fence(*arrived):
        s["held"].update(arrived)
        s.update(lax.optimization_barrier(s))

    def mine(p):
        first = p % 2 * half + p // 2 * e
        s["held"][0, p] = take_rows(s["where"], basis_rows, first, e)

    def fetch4(p):
        return (4, p), lax.ppermute(s["held"][0, p], "blk", below(4))

    def fetch1(p):
        send = jnp.where(column == 0, s["held"][4, p], s["held"][0, p])
        return (1, p), lax.ppermute(send, "blk", around(-1))

    def fetch3(p):
        send = jnp.where(column == RING - 1, s["held"][0, p], s["held"][4, p])
        return (3, p), lax.ppermute(send, "blk", around(1))

    def part(k, j):
        if j is None:
            return [basis_rows]
        return [s["relayed"]] if k == 2 else [s["held"][k, 2 * j], s["held"][k, 2 * j + 1]]

    def partners(*groups):
        return [part(k, j) for group in groups for k, j in group]

    def make(group, into=None, room=None, offset=0):
        into = into or group
        s["made"][into] = handed_products(
            s["handed"], partners(group), group, s["made"].get(into), room, offset
        )

    def finish(theirs, *groups, offset=0):
        s["out"] = kept_products(
            s["out"], weights, s["kept"], theirs, partners(*groups), groups, offset
        )

    own, ones = ((0, None),), ((4, 0), (4, 1), (1, 0), (3, 0))
    twos, threes = ((4, 2), (1, 1), (3, 1)), ((4, 3), (1, 2), (3, 2))
    everything = own + ones + twos + threes
    room = width(everything, half)
    places = [sum(width(group, half) for group in (own, ones, twos, threes)[:n]) for n in range(4)]

    s["held"][0, 0] = basis_rows[:e]
    fence()
    mine(1)
    s["kept"] = lax.dynamic_slice_in_dim(basis_rows, core * half, half, 0)
    s["handed"] = lax.dynamic_slice_in_dim(basis_rows, (1 - core) * half, half, 0)
    pieces = 2 * PARTS
    x = [fetch4(0), fetch4(1)]
    fence(x[0])
    d, u = [fetch1(0)], [fetch3(0)]
    for p in range(pieces - 1):
        if p + 2 < pieces:
            mine(p + 2)
            x.append(fetch4(p + 2))
        if p == 1:
            make(own, everything, room, places[0])
        if p == 3:
            make(ones, everything, room, places[1])
        if p == 5:
            make(twos, everything, room, places[2])
        fence(x[p + 1])
        d.append(fetch1(p + 1))
        u.append(fetch3(p + 1))
        fence(d[p], u[p])

    make(threes, everything, room, places[3])
    some = (0, 1, 2)
    early = [(some, n, (n, 0, 0, e), (0, 0, n * e, (2 + n) * e)) for n in range(2)]
    late = [((3,), n, (0, 0, n * e, (3 + n) * e), (0, 0, n * e, (3 + n) * e)) for n in range(3)]
    late += [((j,), 2, (1, 0, 2 * j * e, (2 * j + 1) * e), (0, e, 2 * j * e, (2 * j + 1) * e)) for j in some]

    def ahead(blocks):
        rows = [part(1, j) for j in range(1 + max(max(parts) for parts, *_ in blocks))]
        others = [part(3, j) for j in range(1 + max(n for _, n, *_ in blocks))]
        theirs = [swap(array) for array in relayed_products(s["where"], rows, others, blocks)]
        return relayed_products(s["where"], rows, others, blocks, theirs)[0]

    s["ahead"] = ahead(early)
    fence(d[-1], u[-1])

    first_sums = lax.ppermute(s["ahead"], "blk", below(-1))
    relayed = lax.ppermute(jnp.concatenate(part(1, 3)), "blk", below(1))
    last_sums = lax.ppermute(ahead(late), "blk", below(-1))
    third, fourth, fifth = ((1, 3),), ((3, 3),), ((2, 3),)
    make(third)
    make(fourth)
    theirs = [swap(s["made"].pop(everything))]
    finish(theirs, own + ones)
    finish(theirs, twos + threes, offset=places[2])
    s["sums"], s["relayed"] = first_sums, relayed
    fence()

    make(fifth)
    theirs = [swap(s["made"].pop(group)) for group in (third, fourth, fifth)]
    finish(theirs, third, fourth, fifth)
    regions = [(0, n * 2 * e, 3 * e, 2 * e, 0, n * half) for n in range(2)]
    out = scaled_write(s["out"], weights, s["sums"], 2, regions)
    regions = [(0, n * 3 * e, e, 3 * e, 3 * e, n * half) for n in range(2)]
    regions += [(e, (2 * j + n) * e, e, e, j * e, n * half + 2 * e) for j in some for n in range(2)]
    out = scaled_write(out, weights, last_sums, 2, regions)
    return out[None]


def solution(mesh):
    return jax.shard_map(
        body,
        mesh=mesh,
        in_specs=(P("blk", "col"), P("blk", None)),
        out_specs=P("blk", None, "col", None),
        check_vma=False,
    )
```

```python
import jax
import jax.numpy as jnp
from jax import lax
from jax.experimental import pallas as pl
from jax.experimental.pallas import tpu as pltpu
from jax.sharding import PartitionSpec as P

RING = 4
PARTS = 4
STRIP = 512
MIB = 1 << 20
SMALL = pl.CostEstimate(flops=1, bytes_accessed=1, transcendentals=0)
VMEM = pl.BlockSpec(memory_space=pltpu.VMEM)
SMEM = pl.BlockSpec(memory_space=pltpu.SMEM)
ANY = pl.BlockSpec(memory_space=pl.ANY)
HBM = pl.BlockSpec(memory_space=pltpu.HBM)
LIMIT = pltpu.CompilerParams(vmem_limit_bytes=12 * MIB)


def product(rows, partner):
    return lax.dot_general(
        rows, partner, (((1,), (1,)), ((), ())), preferred_element_type=jnp.float32
    )


def strips(height, run):
    @pl.loop(0, height // STRIP)
    def _(strip):
        run(pl.ds(pl.multiple_of(strip * STRIP, STRIP), STRIP))


def take_rows(after, own, first, count):
    def kernel(_, own_ref, taken_ref, sem):
        copy = pltpu.make_async_copy(own_ref.at[pl.ds(first, count), :], taken_ref, sem)
        copy.start()
        copy.wait()

    return pl.pallas_call(
        kernel,
        out_shape=jax.ShapeDtypeStruct((count, own.shape[1]), own.dtype),
        in_specs=[SMEM, HBM],
        out_specs=VMEM,
        scratch_shapes=[pltpu.SemaphoreType.DMA],
        compiler_params=LIMIT,
        cost_estimate=SMALL,
    )(after, own)


def columns(group, half):
    e, first = half // PARTS, 0
    for k, part in group:
        count = 2 * half if part is None else 2 * e
        yield k, count, first, [0] if part is None else [part * e, half + part * e]
        first += count


def width(group, half):
    return sum(count for _, count, _, _ in columns(group, half))


def spans(refs, count, e, run):
    if len(refs) > 1 or count == 2 * e:
        run(0, count, lambda: whole(refs))
        return

    @pl.loop(0, count // (2 * e))
    def _(index):
        at = pl.multiple_of(index * 2 * e, 2 * e)
        run(at, 2 * e, lambda: refs[0][pl.ds(at, 2 * e), :])


def whole(refs):
    return refs[0][...] if len(refs) == 1 else jnp.concatenate([ref[...] for ref in refs], axis=0)


def deal(refs, partners):
    refs = iter(refs)
    return [[next(refs) for _ in arrays] for arrays in partners]


def handed_products(handed, partners, group, before=None, room=None, offset=0):
    half, many = handed.shape[0], sum(map(len, partners))
    room = room or width(group, half)

    def kernel(handed_ref, *refs):
        made_ref = refs[-1]
        for (_, count, first, _), tile_refs in zip(columns(group, half), deal(refs, partners)):
            def span(column, columns, partner):
                def strip(at):
                    across = pl.ds(offset + first + column, columns)
                    made_ref[at, across] = product(handed_ref[at, :], partner())
                strips(half, strip)

            spans(tile_refs, count, half // PARTS, span)

    return pl.pallas_call(
        kernel,
        out_shape=jax.ShapeDtypeStruct((half, room), jnp.float32),
        in_specs=[VMEM] * (1 + many) + [VMEM] * (before is not None),
        out_specs=VMEM,
        input_output_aliases={} if before is None else {1 + many: 0},
        compiler_params=LIMIT,
        cost_estimate=SMALL,
    )(handed, *sum(partners, []), *([] if before is None else [before]))


def kept_products(out, weights, kept, theirs, partners, groups, offset=0):
    half, first_call = kept.shape[0], out is None
    many = sum(map(len, partners))

    def kernel(weights_ref, kept_ref, *refs):
        theirs_refs, refs = refs[:len(groups)], refs[len(groups):]
        partner_refs, refs = iter(deal(refs, partners)), refs[many:]
        out_ref, *made_refs, sems = refs if first_call else refs[1:]
        copies = []
        for group, theirs_ref, made_ref in zip(groups, theirs_refs, made_refs):
            for (k, count, first, runs), tile_refs in zip(columns(group, half), partner_refs):
                def span(column, columns, partner):
                    def strip(at):
                        across = pl.ds(first + column, columns)
                        there = pl.ds(offset + first + column, columns)
                        total = product(kept_ref[at, :], partner()) + theirs_ref[at, there]
                        made_ref[at, across] = total * weights_ref[k]
                    strips(half, strip)

                spans(tile_refs, count, half // PARTS, span)
                for n, column in enumerate(runs):
                    run = count // len(runs)
                    copies.append(pltpu.make_async_copy(
                        made_ref.at[:, pl.ds(first + n * run, run)],
                        out_ref.at[k, :, pl.ds(column, run)],
                        sems.at[len(copies)],
                    ))
                    copies[-1].start()
        for copy in copies:
            copy.wait()

    inputs = len(groups) + many
    return pl.pallas_call(
        kernel,
        out_shape=jax.ShapeDtypeStruct((5, half, 2 * half), jnp.float32),
        in_specs=[SMEM] + [VMEM] * (1 + inputs) + [ANY] * (not first_call),
        out_specs=ANY,
        scratch_shapes=[pltpu.VMEM((half, width(group, half)), jnp.float32) for group in groups]
        + [pltpu.SemaphoreType.DMA((2 * sum(map(len, groups)),))],
        input_output_aliases={} if first_call else {2 + inputs: 0},
        compiler_params=LIMIT,
        cost_estimate=SMALL,
    )(weights, kept, *theirs, *sum(partners, []), *([] if first_call else [out]))


def relayed_products(where, rows, partners, blocks, theirs=()):
    e, sums = rows[0][0].shape[0], len(theirs) > 0
    used = sorted({j for parts, *_ in blocks for j in parts})
    sizes = {}
    for parts, _, *places in blocks:
        array, first, *starts = places[sums]
        height, size = sizes.get(array, (0, 0))
        sizes[array] = max(height, first + len(parts) * e), max(size, *(c + e for c in starts))

    def kernel(where_ref, *refs):
        row_refs, refs = deal(refs, rows), refs[2 * len(rows):]
        partner_refs, refs = deal(refs, partners), refs[2 * len(partners):]
        theirs_refs, (*made_refs, taken_ref) = refs[:len(theirs)], refs[len(theirs):]

        def take(kept):
            for n, j in enumerate(used):
                taken_ref[pl.ds(n * e, e), :] = row_refs[j][kept][...]

        for core in range(2):
            pl.when(where_ref[0] == core)(lambda core=core: take(core if sums else 1 - core))

        for parts, partner, *places in blocks:
            taken = taken_ref[pl.ds(used.index(parts[0]) * e, len(parts) * e), :]
            made = product(taken, whole(partner_refs[partner]))
            for n in range(2):
                piece = made[:, n * e:(n + 1) * e]
                if sums:
                    array, first, *starts = places[0]
                    piece += theirs_refs[array][pl.ds(first, len(parts) * e), pl.ds(starts[n], e)]
                array, first, *starts = places[sums]
                made_refs[array][pl.ds(first, len(parts) * e), pl.ds(starts[n], e)] = piece

    operands = sum([*rows, *partners], []) + list(theirs)
    return pl.pallas_call(
        kernel,
        out_shape=[jax.ShapeDtypeStruct(sizes[n], jnp.float32) for n in sorted(sizes)],
        in_specs=[SMEM] + [VMEM] * len(operands),
        out_specs=[VMEM] * len(sizes),
        scratch_shapes=[pltpu.VMEM((len(used) * e, rows[0][0].shape[1]), rows[0][0].dtype)],
        compiler_params=LIMIT,
        cost_estimate=SMALL,
    )(where, *operands)


def scaled_write(out, weights, made, k, regions):
    def kernel(weights_ref, summed_ref, _, out_ref, made_ref, sems):
        made_ref[...] = summed_ref[...] * weights_ref[k]
        copies = [
            pltpu.make_async_copy(
                made_ref.at[pl.ds(row, height), pl.ds(column, size)],
                out_ref.at[k, pl.ds(to_row, height), pl.ds(to_column, size)],
                sems.at[n],
            )
            for n, (row, column, height, size, to_row, to_column) in enumerate(regions)
        ]
        for copy in copies:
            copy.start()
        for copy in copies:
            copy.wait()

    return pl.pallas_call(
        kernel,
        out_shape=jax.ShapeDtypeStruct(out.shape, jnp.float32),
        in_specs=[SMEM, VMEM, ANY],
        out_specs=ANY,
        scratch_shapes=[
            pltpu.VMEM(made.shape, jnp.float32), pltpu.SemaphoreType.DMA((len(regions),))
        ],
        input_output_aliases={2: 0},
        compiler_params=LIMIT,
        cost_estimate=SMALL,
    )(weights, made, out)


def body(basis_rows, screen):
    blocks = lax.axis_size("blk")
    half = basis_rows.shape[0] // 2
    e = half // PARTS
    column = lax.axis_index("blk") % RING
    core = lax.axis_index("col")
    weights = jnp.concatenate([jnp.ones((1,), jnp.float32), screen[0].astype(jnp.float32)])

    def below(distance):
        return [(i, (i - distance) % blocks) for i in range(blocks)]

    def around(distance):
        return [(i, i - i % RING + (i + distance) % RING) for i in range(blocks)]

    def swap(array):
        return lax.ppermute(array, "col", [(0, 1), (1, 0)])

    s = dict(where=core.astype(jnp.int32)[None], held={}, made={}, out=None)

    def fence(*arrived):
        s["held"].update(arrived)
        s.update(lax.optimization_barrier(s))

    def mine(p):
        first = p % 2 * half + p // 2 * e
        s["held"][0, p] = take_rows(s["where"], basis_rows, first, e)

    def fetch4(p):
        return (4, p), lax.ppermute(s["held"][0, p], "blk", below(4))

    def fetch1(p):
        send = jnp.where(column == 0, s["held"][4, p], s["held"][0, p])
        return (1, p), lax.ppermute(send, "blk", around(-1))

    def fetch3(p):
        send = jnp.where(column == RING - 1, s["held"][0, p], s["held"][4, p])
        return (3, p), lax.ppermute(send, "blk", around(1))

    def part(k, j):
        if j is None:
            return [basis_rows]
        return [s["relayed"]] if k == 2 else [s["held"][k, 2 * j], s["held"][k, 2 * j + 1]]

    def partners(*groups):
        return [part(k, j) for group in groups for k, j in group]

    def make(group, *others, into=None, room=None, offset=0):
        for other in others:
            make(other)
        into = into or group
        s["made"][into] = handed_products(
            s["handed"], partners(group), group, s["made"].get(into), room, offset
        )

    def finish(theirs, *groups, offset=0):
        s["out"] = kept_products(
            s["out"], weights, s["kept"], theirs, partners(*groups), groups, offset
        )

    own, ones = ((0, None),), ((4, 0), (4, 1), (1, 0), (3, 0))
    twos, threes = ((4, 2), (1, 1), (3, 1)), ((4, 3), (1, 2), (3, 2))
    everything = own + ones + twos + threes
    room = width(everything, half)
    places = [sum(width(group, half) for group in (own, ones, twos, threes)[:n]) for n in range(4)]

    s["held"][0, 0] = basis_rows[:e]
    fence()
    mine(1)
    s["kept"] = lax.dynamic_slice_in_dim(basis_rows, core * half, half, 0)
    s["handed"] = lax.dynamic_slice_in_dim(basis_rows, (1 - core) * half, half, 0)
    pieces = 2 * PARTS
    x = [fetch4(0), fetch4(1)]
    fence(x[0])
    d, u = [fetch1(0)], [fetch3(0)]
    for p in range(pieces - 1):
        if p + 2 < pieces:
            mine(p + 2)
            x.append(fetch4(p + 2))
        if p == 1:
            make(own, into=everything, room=room, offset=places[0])
        if p == 3:
            make(ones, into=everything, room=room, offset=places[1])
        if p == 5:
            make(twos, into=everything, room=room, offset=places[2])
        fence(x[p + 1])
        d.append(fetch1(p + 1))
        u.append(fetch3(p + 1))
        fence(d[p], u[p])

    make(threes, into=everything, room=room, offset=places[3])
    some = (0, 1, 2)
    early = [(some, n, (n, 0, 0, e), (0, 0, n * e, (2 + n) * e)) for n in range(2)]
    late = [((3,), n, (0, 0, n * e, (3 + n) * e), (0, 0, n * e, (3 + n) * e)) for n in range(3)]
    late += [((j,), 2, (1, 0, 2 * j * e, (2 * j + 1) * e), (0, e, 2 * j * e, (2 * j + 1) * e)) for j in some]

    def ahead(blocks, *meanwhile):
        rows = [part(1, j) for j in range(1 + max(max(parts) for parts, *_ in blocks))]
        others = [part(3, j) for j in range(1 + max(n for _, n, *_ in blocks))]
        theirs = [swap(array) for array in relayed_products(s["where"], rows, others, blocks)]
        if meanwhile:
            make(*meanwhile)
            fresh = {group: s["made"][group] for group in meanwhile}
            theirs, fresh = lax.optimization_barrier((theirs, fresh))
            s["made"].update(fresh)
        return relayed_products(s["where"], rows, others, blocks, theirs)[0]

    s["ahead"] = ahead(early)
    fence(d[-1], u[-1])

    first_sums = lax.ppermute(s["ahead"], "blk", below(-1))
    relayed = lax.ppermute(jnp.concatenate(part(1, 3)), "blk", below(1))
    third, fourth, fifth = ((1, 3),), ((3, 3),), ((2, 3),)
    last_sums = lax.ppermute(ahead(late, third, fourth), "blk", below(-1))
    theirs = [swap(s["made"].pop(everything))]
    finish(theirs, own + ones)
    finish(theirs, twos + threes, offset=places[2])
    s["sums"], s["relayed"] = first_sums, relayed
    fence()

    make(fifth)
    regions = [(0, n * 2 * e, 3 * e, 2 * e, 0, n * half) for n in range(2)]
    s["out"] = scaled_write(s["out"], weights, s["sums"], 2, regions)
    theirs = [swap(s["made"].pop(group)) for group in (third, fourth, fifth)]
    finish(theirs, third, fourth, fifth)
    regions = [(0, n * 3 * e, e, 3 * e, 3 * e, n * half) for n in range(2)]
    regions += [(e, (2 * j + n) * e, e, e, j * e, n * half + 2 * e) for j in some for n in range(2)]
    out = scaled_write(s["out"], weights, last_sums, 2, regions)
    return out[None]


def solution(mesh):
    return jax.shard_map(
        body,
        mesh=mesh,
        in_specs=(P("blk", "col"), P("blk", None)),
        out_specs=P("blk", None, "col", None),
        check_vma=False,
    )
```

```python
import jax
import jax.numpy as jnp
from jax import lax
from jax.experimental import pallas as pl
from jax.experimental.pallas import tpu as pltpu
from jax.sharding import PartitionSpec as P

RING = 4
PARTS = 4
STRIP = 512
MIB = 1 << 20
SMALL = pl.CostEstimate(flops=1, bytes_accessed=1, transcendentals=0)
VMEM = pl.BlockSpec(memory_space=pltpu.VMEM)
SMEM = pl.BlockSpec(memory_space=pltpu.SMEM)
ANY = pl.BlockSpec(memory_space=pl.ANY)
HBM = pl.BlockSpec(memory_space=pltpu.HBM)
LIMIT = pltpu.CompilerParams(vmem_limit_bytes=12 * MIB)


def product(rows, partner):
    return lax.dot_general(
        rows, partner, (((1,), (1,)), ((), ())), preferred_element_type=jnp.float32
    )


def strips(height, run):
    @pl.loop(0, height // STRIP)
    def _(strip):
        run(pl.ds(pl.multiple_of(strip * STRIP, STRIP), STRIP))


def take_rows(after, own, first, count):
    def kernel(_, own_ref, taken_ref, sem):
        copy = pltpu.make_async_copy(own_ref.at[pl.ds(first, count), :], taken_ref, sem)
        copy.start()
        copy.wait()

    return pl.pallas_call(
        kernel,
        out_shape=jax.ShapeDtypeStruct((count, own.shape[1]), own.dtype),
        in_specs=[SMEM, HBM],
        out_specs=VMEM,
        scratch_shapes=[pltpu.SemaphoreType.DMA],
        compiler_params=LIMIT,
        cost_estimate=SMALL,
    )(after, own)


def rows_to_send(place, received, mine):
    def kernel(place_ref, received_ref, mine_ref, down_ref, up_ref, sems):
        def send(chosen, to_ref, n, act):
            for ref, use in ((received_ref, chosen), (mine_ref, jnp.logical_not(chosen))):
                pl.when(use)(lambda ref=ref: act(pltpu.make_async_copy(ref, to_ref, sems.at[n])))

        passed_down, passed_up = place_ref[0] == 0, place_ref[0] != RING - 1
        for act in (lambda copy: copy.start(), lambda copy: copy.wait()):
            send(passed_down, down_ref, 0, act)
            send(passed_up, up_ref, 1, act)

    return pl.pallas_call(
        kernel,
        out_shape=[jax.ShapeDtypeStruct(mine.shape, mine.dtype)] * 2,
        in_specs=[SMEM, ANY, ANY],
        out_specs=[HBM, HBM],
        scratch_shapes=[pltpu.SemaphoreType.DMA((2,))],
        compiler_params=LIMIT,
        cost_estimate=SMALL,
    )(place, received, mine)


def columns(group, half):
    e, first = half // PARTS, 0
    for k, part in group:
        count = 2 * half if part is None else 2 * e
        yield k, count, first, [0] if part is None else [part * e, half + part * e]
        first += count


def width(group, half):
    return sum(count for _, count, _, _ in columns(group, half))


def spans(refs, count, e, run):
    if len(refs) > 1 or count == 2 * e:
        run(0, count, lambda: whole(refs))
        return

    @pl.loop(0, count // (2 * e))
    def _(index):
        at = pl.multiple_of(index * 2 * e, 2 * e)
        run(at, 2 * e, lambda: refs[0][pl.ds(at, 2 * e), :])


def whole(refs):
    return refs[0][...] if len(refs) == 1 else jnp.concatenate([ref[...] for ref in refs], axis=0)


def deal(refs, partners):
    refs = iter(refs)
    return [[next(refs) for _ in arrays] for arrays in partners]


def handed_products(handed, partners, group, before=None, room=None, offset=0):
    half, many = handed.shape[0], sum(map(len, partners))
    room = room or width(group, half)

    def kernel(handed_ref, *refs):
        made_ref = refs[-1]
        for (_, count, first, _), tile_refs in zip(columns(group, half), deal(refs, partners)):
            def span(column, columns, partner):
                def strip(at):
                    across = pl.ds(offset + first + column, columns)
                    made_ref[at, across] = product(handed_ref[at, :], partner())
                strips(half, strip)

            spans(tile_refs, count, half // PARTS, span)

    return pl.pallas_call(
        kernel,
        out_shape=jax.ShapeDtypeStruct((half, room), jnp.float32),
        in_specs=[VMEM] * (1 + many) + [VMEM] * (before is not None),
        out_specs=VMEM,
        input_output_aliases={} if before is None else {1 + many: 0},
        compiler_params=LIMIT,
        cost_estimate=SMALL,
    )(handed, *sum(partners, []), *([] if before is None else [before]))


def kept_products(out, weights, kept, theirs, partners, groups, offset=0):
    half, first_call = kept.shape[0], out is None
    many = sum(map(len, partners))

    def kernel(weights_ref, kept_ref, *refs):
        theirs_refs, refs = refs[:len(groups)], refs[len(groups):]
        partner_refs, refs = iter(deal(refs, partners)), refs[many:]
        out_ref, *made_refs, sems = refs if first_call else refs[1:]
        copies = []
        for group, theirs_ref, made_ref in zip(groups, theirs_refs, made_refs):
            for (k, count, first, runs), tile_refs in zip(columns(group, half), partner_refs):
                def span(column, columns, partner):
                    def strip(at):
                        across = pl.ds(first + column, columns)
                        there = pl.ds(offset + first + column, columns)
                        total = product(kept_ref[at, :], partner()) + theirs_ref[at, there]
                        made_ref[at, across] = total * weights_ref[k]
                    strips(half, strip)

                spans(tile_refs, count, half // PARTS, span)
                for n, column in enumerate(runs):
                    run = count // len(runs)
                    copies.append(pltpu.make_async_copy(
                        made_ref.at[:, pl.ds(first + n * run, run)],
                        out_ref.at[k, :, pl.ds(column, run)],
                        sems.at[len(copies)],
                    ))
                    copies[-1].start()
        for copy in copies:
            copy.wait()

    inputs = len(groups) + many
    return pl.pallas_call(
        kernel,
        out_shape=jax.ShapeDtypeStruct((5, half, 2 * half), jnp.float32),
        in_specs=[SMEM] + [VMEM] * (1 + inputs) + [ANY] * (not first_call),
        out_specs=ANY,
        scratch_shapes=[pltpu.VMEM((half, width(group, half)), jnp.float32) for group in groups]
        + [pltpu.SemaphoreType.DMA((2 * sum(map(len, groups)),))],
        input_output_aliases={} if first_call else {2 + inputs: 0},
        compiler_params=LIMIT,
        cost_estimate=SMALL,
    )(weights, kept, *theirs, *sum(partners, []), *([] if first_call else [out]))


def relayed_products(where, rows, partners, blocks, theirs=()):
    e, sums = rows[0][0].shape[0], len(theirs) > 0
    used = sorted({j for parts, *_ in blocks for j in parts})
    sizes = {}
    for parts, _, *places in blocks:
        array, first, *starts = places[sums]
        height, size = sizes.get(array, (0, 0))
        sizes[array] = max(height, first + len(parts) * e), max(size, *(c + e for c in starts))

    def kernel(where_ref, *refs):
        row_refs, refs = deal(refs, rows), refs[2 * len(rows):]
        partner_refs, refs = deal(refs, partners), refs[2 * len(partners):]
        theirs_refs, (*made_refs, taken_ref) = refs[:len(theirs)], refs[len(theirs):]

        def take(kept):
            for n, j in enumerate(used):
                taken_ref[pl.ds(n * e, e), :] = row_refs[j][kept][...]

        for core in range(2):
            pl.when(where_ref[0] == core)(lambda core=core: take(core if sums else 1 - core))

        for parts, partner, *places in blocks:
            taken = taken_ref[pl.ds(used.index(parts[0]) * e, len(parts) * e), :]
            made = product(taken, whole(partner_refs[partner]))
            for n in range(2):
                piece = made[:, n * e:(n + 1) * e]
                if sums:
                    array, first, *starts = places[0]
                    piece += theirs_refs[array][pl.ds(first, len(parts) * e), pl.ds(starts[n], e)]
                array, first, *starts = places[sums]
                made_refs[array][pl.ds(first, len(parts) * e), pl.ds(starts[n], e)] = piece

    operands = sum([*rows, *partners], []) + list(theirs)
    return pl.pallas_call(
        kernel,
        out_shape=[jax.ShapeDtypeStruct(sizes[n], jnp.float32) for n in sorted(sizes)],
        in_specs=[SMEM] + [VMEM] * len(operands),
        out_specs=[VMEM] * len(sizes),
        scratch_shapes=[pltpu.VMEM((len(used) * e, rows[0][0].shape[1]), rows[0][0].dtype)],
        compiler_params=LIMIT,
        cost_estimate=SMALL,
    )(where, *operands)


def scaled_write(out, weights, made, k, regions):
    def kernel(weights_ref, summed_ref, _, out_ref, made_ref, sems):
        made_ref[...] = summed_ref[...] * weights_ref[k]
        copies = [
            pltpu.make_async_copy(
                made_ref.at[pl.ds(row, height), pl.ds(column, size)],
                out_ref.at[k, pl.ds(to_row, height), pl.ds(to_column, size)],
                sems.at[n],
            )
            for n, (row, column, height, size, to_row, to_column) in enumerate(regions)
        ]
        for copy in copies:
            copy.start()
        for copy in copies:
            copy.wait()

    return pl.pallas_call(
        kernel,
        out_shape=jax.ShapeDtypeStruct(out.shape, jnp.float32),
        in_specs=[SMEM, VMEM, ANY],
        out_specs=ANY,
        scratch_shapes=[
            pltpu.VMEM(made.shape, jnp.float32), pltpu.SemaphoreType.DMA((len(regions),))
        ],
        input_output_aliases={2: 0},
        compiler_params=LIMIT,
        cost_estimate=SMALL,
    )(weights, made, out)


def body(basis_rows, screen):
    blocks = lax.axis_size("blk")
    half = basis_rows.shape[0] // 2
    e = half // PARTS
    column = lax.axis_index("blk") % RING
    core = lax.axis_index("col")
    weights = jnp.concatenate([jnp.ones((1,), jnp.float32), screen[0].astype(jnp.float32)])

    def below(distance):
        return [(i, (i - distance) % blocks) for i in range(blocks)]

    def around(distance):
        return [(i, i - i % RING + (i + distance) % RING) for i in range(blocks)]

    def swap(array):
        return lax.ppermute(array, "col", [(0, 1), (1, 0)])

    place = column.astype(jnp.int32)[None]
    s = dict(where=core.astype(jnp.int32)[None], place=place, held={}, made={}, out=None)

    def fence(*arrived):
        s["held"].update(arrived)
        s.update(lax.optimization_barrier(s))

    def mine(p):
        first = p % 2 * half + p // 2 * e
        s["held"][0, p] = take_rows(s["where"], basis_rows, first, e)

    def fetch4(p):
        return (4, p), lax.ppermute(s["held"][0, p], "blk", below(4))

    def fetch13(p):
        down, up = rows_to_send(s["place"], s["held"][4, p], s["held"][0, p])
        d.append(((1, p), lax.ppermute(down, "blk", around(-1))))
        u.append(((3, p), lax.ppermute(up, "blk", around(1))))

    def part(k, j):
        if j is None:
            return [basis_rows]
        return [s["relayed"]] if k == 2 else [s["held"][k, 2 * j], s["held"][k, 2 * j + 1]]

    def partners(*groups):
        return [part(k, j) for group in groups for k, j in group]

    def make(group, *others, into=None, room=None, offset=0):
        for other in others:
            make(other)
        into = into or group
        s["made"][into] = handed_products(
            s["handed"], partners(group), group, s["made"].get(into), room, offset
        )

    def finish(theirs, *groups, offset=0):
        s["out"] = kept_products(
            s["out"], weights, s["kept"], theirs, partners(*groups), groups, offset
        )

    own, ones = ((0, None),), ((4, 0), (4, 1), (1, 0), (3, 0))
    twos, threes = ((4, 2), (1, 1), (3, 1)), ((4, 3), (1, 2), (3, 2))
    everything = own + ones + twos + threes
    room = width(everything, half)
    places = [sum(width(group, half) for group in (own, ones, twos, threes)[:n]) for n in range(4)]

    s["held"][0, 0] = basis_rows[:e]
    fence()
    mine(1)
    s["kept"] = lax.dynamic_slice_in_dim(basis_rows, core * half, half, 0)
    s["handed"] = lax.dynamic_slice_in_dim(basis_rows, (1 - core) * half, half, 0)
    pieces = 2 * PARTS
    x = [fetch4(0), fetch4(1)]
    fence(x[0])
    d, u = [], []
    fetch13(0)
    for p in range(pieces - 1):
        if p + 2 < pieces:
            mine(p + 2)
            x.append(fetch4(p + 2))
        if p == 1:
            make(own, into=everything, room=room, offset=places[0])
        if p == 3:
            make(ones, into=everything, room=room, offset=places[1])
        if p == 5:
            make(twos, into=everything, room=room, offset=places[2])
        fence(x[p + 1])
        fetch13(p + 1)
        fence(d[p], u[p])

    make(threes, into=everything, room=room, offset=places[3])
    some = (0, 1, 2)
    early = [(some, n, (n, 0, 0, e), (0, 0, n * e, (2 + n) * e)) for n in range(2)]
    late = [((3,), n, (0, 0, n * e, (3 + n) * e), (0, 0, n * e, (3 + n) * e)) for n in range(3)]
    late += [((j,), 2, (1, 0, 2 * j * e, (2 * j + 1) * e), (0, e, 2 * j * e, (2 * j + 1) * e)) for j in some]

    def ahead(blocks, *meanwhile):
        rows = [part(1, j) for j in range(1 + max(max(parts) for parts, *_ in blocks))]
        others = [part(3, j) for j in range(1 + max(n for _, n, *_ in blocks))]
        theirs = [swap(array) for array in relayed_products(s["where"], rows, others, blocks)]
        if meanwhile:
            make(*meanwhile)
            fresh = {group: s["made"][group] for group in meanwhile}
            theirs, fresh = lax.optimization_barrier((theirs, fresh))
            s["made"].update(fresh)
        return relayed_products(s["where"], rows, others, blocks, theirs)[0]

    s["ahead"] = ahead(early)
    fence(d[-1], u[-1])

    first_sums = lax.ppermute(s["ahead"], "blk", below(-1))
    relayed = lax.ppermute(jnp.concatenate(part(1, 3)), "blk", below(1))
    third, fourth, fifth = ((1, 3),), ((3, 3),), ((2, 3),)
    last_sums = lax.ppermute(ahead(late, third, fourth), "blk", below(-1))
    theirs = [swap(s["made"].pop(everything))]
    finish(theirs, own + ones)
    finish(theirs, twos + threes, offset=places[2])
    s["sums"], s["relayed"] = first_sums, relayed
    fence()

    make(fifth)
    regions = [(0, n * 2 * e, 3 * e, 2 * e, 0, n * half) for n in range(2)]
    s["out"] = scaled_write(s["out"], weights, s["sums"], 2, regions)
    theirs = [swap(s["made"].pop(group)) for group in (third, fourth, fifth)]
    finish(theirs, third, fourth, fifth)
    regions = [(0, n * 3 * e, e, 3 * e, 3 * e, n * half) for n in range(2)]
    regions += [(e, (2 * j + n) * e, e, e, j * e, n * half + 2 * e) for j in some for n in range(2)]
    out = scaled_write(s["out"], weights, last_sums, 2, regions)
    return out[None]


def solution(mesh):
    return jax.shard_map(
        body,
        mesh=mesh,
        in_specs=(P("blk", "col"), P("blk", None)),
        out_specs=P("blk", None, "col", None),
        check_vma=False,
    )
```

```python
import jax
import jax.numpy as jnp
from jax import lax
from jax.experimental import pallas as pl
from jax.experimental.pallas import tpu as pltpu
from jax.sharding import PartitionSpec as P

RING = 4
PARTS = 4
STRIP = 512
MIB = 1 << 20
SMALL = pl.CostEstimate(flops=1, bytes_accessed=1, transcendentals=0)
VMEM = pl.BlockSpec(memory_space=pltpu.VMEM)
SMEM = pl.BlockSpec(memory_space=pltpu.SMEM)
ANY = pl.BlockSpec(memory_space=pl.ANY)
HBM = pl.BlockSpec(memory_space=pltpu.HBM)
LIMIT = pltpu.CompilerParams(vmem_limit_bytes=12 * MIB)


def product(rows, partner):
    return lax.dot_general(
        rows, partner, (((1,), (1,)), ((), ())), preferred_element_type=jnp.float32
    )


def strips(height, run):
    @pl.loop(0, height // STRIP)
    def _(strip):
        run(pl.ds(pl.multiple_of(strip * STRIP, STRIP), STRIP))


def take_rows(after, own, first, count):
    def kernel(_, own_ref, taken_ref, sem):
        copy = pltpu.make_async_copy(own_ref.at[pl.ds(first, count), :], taken_ref, sem)
        copy.start()
        copy.wait()

    return pl.pallas_call(
        kernel,
        out_shape=jax.ShapeDtypeStruct((count, own.shape[1]), own.dtype),
        in_specs=[SMEM, HBM],
        out_specs=VMEM,
        scratch_shapes=[pltpu.SemaphoreType.DMA],
        compiler_params=LIMIT,
        cost_estimate=SMALL,
    )(after, own)


def rows_to_send(place, received, mine):
    def kernel(place_ref, received_ref, mine_ref, up_ref, down_ref, sems):
        def send(chosen, to_ref, n, act):
            for ref, use in ((received_ref, chosen), (mine_ref, jnp.logical_not(chosen))):
                pl.when(use)(lambda ref=ref: act(pltpu.make_async_copy(ref, to_ref, sems.at[n])))

        passed_down, passed_up = place_ref[0] == 0, place_ref[0] != RING - 1
        for act in (lambda copy: copy.start(), lambda copy: copy.wait()):
            send(passed_down, down_ref, 0, act)
            send(passed_up, up_ref, 1, act)

    return pl.pallas_call(
        kernel,
        out_shape=[jax.ShapeDtypeStruct(mine.shape, mine.dtype)] * 2,
        in_specs=[SMEM, ANY, ANY],
        out_specs=[HBM, HBM],
        scratch_shapes=[pltpu.SemaphoreType.DMA((2,))],
        compiler_params=LIMIT,
        cost_estimate=SMALL,
    )(place, received, mine)


def columns(group, half):
    e, first = half // PARTS, 0
    for k, part in group:
        count = 2 * half if part is None else 2 * e
        yield k, count, first, [0] if part is None else [part * e, half + part * e]
        first += count


def width(group, half):
    return sum(count for _, count, _, _ in columns(group, half))


def spans(refs, count, e, run):
    if len(refs) > 1 or count == 2 * e:
        run(0, count, lambda: whole(refs))
        return

    @pl.loop(0, count // (2 * e))
    def _(index):
        at = pl.multiple_of(index * 2 * e, 2 * e)
        run(at, 2 * e, lambda: refs[0][pl.ds(at, 2 * e), :])


def whole(refs):
    return refs[0][...] if len(refs) == 1 else jnp.concatenate([ref[...] for ref in refs], axis=0)


def deal(refs, partners):
    refs = iter(refs)
    return [[next(refs) for _ in arrays] for arrays in partners]


def handed_products(handed, partners, group, before=None, room=None, offset=0):
    half, many = handed.shape[0], sum(map(len, partners))
    room = room or width(group, half)

    def kernel(handed_ref, *refs):
        made_ref = refs[-1]
        for (_, count, first, _), tile_refs in zip(columns(group, half), deal(refs, partners)):
            def span(column, columns, partner):
                def strip(at):
                    across = pl.ds(offset + first + column, columns)
                    made_ref[at, across] = product(handed_ref[at, :], partner())
                strips(half, strip)

            spans(tile_refs, count, half // PARTS, span)

    return pl.pallas_call(
        kernel,
        out_shape=jax.ShapeDtypeStruct((half, room), jnp.float32),
        in_specs=[VMEM] * (1 + many) + [VMEM] * (before is not None),
        out_specs=VMEM,
        input_output_aliases={} if before is None else {1 + many: 0},
        compiler_params=LIMIT,
        cost_estimate=SMALL,
    )(handed, *sum(partners, []), *([] if before is None else [before]))


def kept_products(out, weights, kept, theirs, partners, groups, offset=0):
    half, first_call = kept.shape[0], out is None
    many = sum(map(len, partners))

    def kernel(weights_ref, kept_ref, *refs):
        theirs_refs, refs = refs[:len(groups)], refs[len(groups):]
        partner_refs, refs = iter(deal(refs, partners)), refs[many:]
        out_ref, *made_refs, sems = refs if first_call else refs[1:]
        copies = []
        for group, theirs_ref, made_ref in zip(groups, theirs_refs, made_refs):
            for (k, count, first, runs), tile_refs in zip(columns(group, half), partner_refs):
                def span(column, columns, partner):
                    def strip(at):
                        across = pl.ds(first + column, columns)
                        there = pl.ds(offset + first + column, columns)
                        total = product(kept_ref[at, :], partner()) + theirs_ref[at, there]
                        made_ref[at, across] = total * weights_ref[k]
                    strips(half, strip)

                spans(tile_refs, count, half // PARTS, span)
                for n, column in enumerate(runs):
                    run = count // len(runs)
                    copies.append(pltpu.make_async_copy(
                        made_ref.at[:, pl.ds(first + n * run, run)],
                        out_ref.at[k, :, pl.ds(column, run)],
                        sems.at[len(copies)],
                    ))
                    copies[-1].start()
        for copy in copies:
            copy.wait()

    inputs = len(groups) + many
    return pl.pallas_call(
        kernel,
        out_shape=jax.ShapeDtypeStruct((5, half, 2 * half), jnp.float32),
        in_specs=[SMEM] + [VMEM] * (1 + inputs) + [ANY] * (not first_call),
        out_specs=ANY,
        scratch_shapes=[pltpu.VMEM((half, width(group, half)), jnp.float32) for group in groups]
        + [pltpu.SemaphoreType.DMA((2 * sum(map(len, groups)),))],
        input_output_aliases={} if first_call else {2 + inputs: 0},
        compiler_params=LIMIT,
        cost_estimate=SMALL,
    )(weights, kept, *theirs, *sum(partners, []), *([] if first_call else [out]))


def relayed_products(where, rows, partners, blocks, theirs=()):
    e, sums = rows[0][0].shape[0], len(theirs) > 0
    used = sorted({j for parts, *_ in blocks for j in parts})
    sizes = {}
    for parts, _, *places in blocks:
        array, first, *starts = places[sums]
        height, size = sizes.get(array, (0, 0))
        sizes[array] = max(height, first + len(parts) * e), max(size, *(c + e for c in starts))

    def kernel(where_ref, *refs):
        row_refs, refs = deal(refs, rows), refs[2 * len(rows):]
        partner_refs, refs = deal(refs, partners), refs[2 * len(partners):]
        theirs_refs, (*made_refs, taken_ref) = refs[:len(theirs)], refs[len(theirs):]

        def take(kept):
            for n, j in enumerate(used):
                taken_ref[pl.ds(n * e, e), :] = row_refs[j][kept][...]

        for core in range(2):
            pl.when(where_ref[0] == core)(lambda core=core: take(core if sums else 1 - core))

        for parts, partner, *places in blocks:
            taken = taken_ref[pl.ds(used.index(parts[0]) * e, len(parts) * e), :]
            made = product(taken, whole(partner_refs[partner]))
            for n in range(2):
                piece = made[:, n * e:(n + 1) * e]
                if sums:
                    array, first, *starts = places[0]
                    piece += theirs_refs[array][pl.ds(first, len(parts) * e), pl.ds(starts[n], e)]
                array, first, *starts = places[sums]
                made_refs[array][pl.ds(first, len(parts) * e), pl.ds(starts[n], e)] = piece

    operands = sum([*rows, *partners], []) + list(theirs)
    return pl.pallas_call(
        kernel,
        out_shape=[jax.ShapeDtypeStruct(sizes[n], jnp.float32) for n in sorted(sizes)],
        in_specs=[SMEM] + [VMEM] * len(operands),
        out_specs=[VMEM] * len(sizes),
        scratch_shapes=[pltpu.VMEM((len(used) * e, rows[0][0].shape[1]), rows[0][0].dtype)],
        compiler_params=LIMIT,
        cost_estimate=SMALL,
    )(where, *operands)


def scaled_write(out, weights, made, k, regions):
    def kernel(weights_ref, summed_ref, _, out_ref, made_ref, sems):
        made_ref[...] = summed_ref[...] * weights_ref[k]
        copies = [
            pltpu.make_async_copy(
                made_ref.at[pl.ds(row, height), pl.ds(column, size)],
                out_ref.at[k, pl.ds(to_row, height), pl.ds(to_column, size)],
                sems.at[n],
            )
            for n, (row, column, height, size, to_row, to_column) in enumerate(regions)
        ]
        for copy in copies:
            copy.start()
        for copy in copies:
            copy.wait()

    return pl.pallas_call(
        kernel,
        out_shape=jax.ShapeDtypeStruct(out.shape, jnp.float32),
        in_specs=[SMEM, VMEM, ANY],
        out_specs=ANY,
        scratch_shapes=[
            pltpu.VMEM(made.shape, jnp.float32), pltpu.SemaphoreType.DMA((len(regions),))
        ],
        input_output_aliases={2: 0},
        compiler_params=LIMIT,
        cost_estimate=SMALL,
    )(weights, made, out)


def body(basis_rows, screen):
    blocks = lax.axis_size("blk")
    half = basis_rows.shape[0] // 2
    e = half // PARTS
    column = lax.axis_index("blk") % RING
    core = lax.axis_index("col")
    weights = jnp.concatenate([jnp.ones((1,), jnp.float32), screen[0].astype(jnp.float32)])

    def below(distance):
        return [(i, (i - distance) % blocks) for i in range(blocks)]

    def around(distance):
        return [(i, i - i % RING + (i + distance) % RING) for i in range(blocks)]

    def swap(array):
        return lax.ppermute(array, "col", [(0, 1), (1, 0)])

    place = column.astype(jnp.int32)[None]
    s = dict(where=core.astype(jnp.int32)[None], place=place, held={}, made={}, out=None)

    def fence(*arrived):
        s["held"].update(arrived)
        s.update(lax.optimization_barrier(s))

    def mine(p):
        first = p % 2 * half + p // 2 * e
        s["held"][0, p] = take_rows(s["where"], basis_rows, first, e)

    def fetch4(p):
        return (4, p), lax.ppermute(s["held"][0, p], "blk", below(4))

    def fetch13(p):
        up, down = rows_to_send(s["place"], s["held"][4, p], s["held"][0, p])
        u.append(((3, p), lax.ppermute(up, "blk", around(1))))
        d.append(((1, p), lax.ppermute(down, "blk", around(-1))))

    def part(k, j):
        if j is None:
            return [basis_rows]
        return [s["relayed"]] if k == 2 else [s["held"][k, 2 * j], s["held"][k, 2 * j + 1]]

    def partners(*groups):
        return [part(k, j) for group in groups for k, j in group]

    def make(group, *others, into=None, room=None, offset=0):
        for other in others:
            make(other)
        into = into or group
        s["made"][into] = handed_products(
            s["handed"], partners(group), group, s["made"].get(into), room, offset
        )

    def finish(theirs, *groups, offset=0):
        s["out"] = kept_products(
            s["out"], weights, s["kept"], theirs, partners(*groups), groups, offset
        )

    own, ones = ((0, None),), ((4, 0), (4, 1), (1, 0), (3, 0))
    twos, threes = ((4, 2), (1, 1), (3, 1)), ((4, 3), (1, 2), (3, 2))
    everything = own + ones + twos + threes
    room = width(everything, half)
    places = [sum(width(group, half) for group in (own, ones, twos, threes)[:n]) for n in range(4)]

    s["held"][0, 0] = basis_rows[:e]
    fence()
    mine(1)
    s["kept"] = lax.dynamic_slice_in_dim(basis_rows, core * half, half, 0)
    s["handed"] = lax.dynamic_slice_in_dim(basis_rows, (1 - core) * half, half, 0)
    pieces = 2 * PARTS
    x = [fetch4(0), fetch4(1)]
    fence(x[0])
    d, u = [], []
    fetch13(0)
    for p in range(pieces - 1):
        if p + 2 < pieces:
            mine(p + 2)
            x.append(fetch4(p + 2))
        if p == 1:
            make(own, into=everything, room=room, offset=places[0])
        if p == 3:
            make(ones, into=everything, room=room, offset=places[1])
        if p == 5:
            make(twos, into=everything, room=room, offset=places[2])
        fence(x[p + 1])
        fetch13(p + 1)
        fence(u[p])
        fence(d[p])

    make(threes, into=everything, room=room, offset=places[3])
    some = (0, 1, 2)
    early = [(some, n, (n, 0, 0, e), (0, 0, n * e, (2 + n) * e)) for n in range(2)]
    late = [((3,), n, (0, 0, n * e, (3 + n) * e), (0, 0, n * e, (3 + n) * e)) for n in range(3)]
    late += [((j,), 2, (1, 0, 2 * j * e, (2 * j + 1) * e), (0, e, 2 * j * e, (2 * j + 1) * e)) for j in some]

    def ahead(blocks, *meanwhile):
        rows = [part(1, j) for j in range(1 + max(max(parts) for parts, *_ in blocks))]
        others = [part(3, j) for j in range(1 + max(n for _, n, *_ in blocks))]
        theirs = [swap(array) for array in relayed_products(s["where"], rows, others, blocks)]
        if meanwhile:
            make(*meanwhile)
            fresh = {group: s["made"][group] for group in meanwhile}
            theirs, fresh = lax.optimization_barrier((theirs, fresh))
            s["made"].update(fresh)
        return relayed_products(s["where"], rows, others, blocks, theirs)[0]

    s["ahead"] = ahead(early)
    fence(u[-1])
    fence(d[-1])

    first_sums = lax.ppermute(s["ahead"], "blk", below(-1))
    relayed = lax.ppermute(jnp.concatenate(part(1, 3)), "blk", below(1))
    third, fourth, fifth = ((1, 3),), ((3, 3),), ((2, 3),)
    last_sums = lax.ppermute(ahead(late, third, fourth), "blk", below(-1))
    theirs = [swap(s["made"].pop(everything))]
    finish(theirs, own + ones)
    finish(theirs, twos + threes, offset=places[2])
    s["sums"], s["relayed"] = first_sums, relayed
    fence()

    make(fifth)
    regions = [(0, n * 2 * e, 3 * e, 2 * e, 0, n * half) for n in range(2)]
    s["out"] = scaled_write(s["out"], weights, s["sums"], 2, regions)
    theirs = [swap(s["made"].pop(group)) for group in (third, fourth, fifth)]
    finish(theirs, third, fourth, fifth)
    regions = [(0, n * 3 * e, e, 3 * e, 3 * e, n * half) for n in range(2)]
    regions += [(e, (2 * j + n) * e, e, e, j * e, n * half + 2 * e) for j in some for n in range(2)]
    out = scaled_write(s["out"], weights, last_sums, 2, regions)
    return out[None]


def solution(mesh):
    return jax.shard_map(
        body,
        mesh=mesh,
        in_specs=(P("blk", "col"), P("blk", None)),
        out_specs=P("blk", None, "col", None),
        check_vma=False,
    )
```

```python
import jax
import jax.numpy as jnp
from jax import lax
from jax.experimental import pallas as pl
from jax.experimental.pallas import tpu as pltpu
from jax.sharding import PartitionSpec as P

RING = 4
PARTS = 4
STRIP = 512
MIB = 1 << 20
SMALL = pl.CostEstimate(flops=1, bytes_accessed=1, transcendentals=0)
VMEM = pl.BlockSpec(memory_space=pltpu.VMEM)
SMEM = pl.BlockSpec(memory_space=pltpu.SMEM)
ANY = pl.BlockSpec(memory_space=pl.ANY)
HBM = pl.BlockSpec(memory_space=pltpu.HBM)
LIMIT = pltpu.CompilerParams(vmem_limit_bytes=12 * MIB)


def product(rows, partner):
    return lax.dot_general(
        rows, partner, (((1,), (1,)), ((), ())), preferred_element_type=jnp.float32
    )


def strips(height, run):
    @pl.loop(0, height // STRIP)
    def _(strip):
        run(pl.ds(pl.multiple_of(strip * STRIP, STRIP), STRIP))


def take_rows(after, own, first, count):
    def kernel(_, own_ref, taken_ref, sem):
        copy = pltpu.make_async_copy(own_ref.at[pl.ds(first, count), :], taken_ref, sem)
        copy.start()
        copy.wait()

    return pl.pallas_call(
        kernel,
        out_shape=jax.ShapeDtypeStruct((count, own.shape[1]), own.dtype),
        in_specs=[SMEM, HBM],
        out_specs=VMEM,
        scratch_shapes=[pltpu.SemaphoreType.DMA],
        compiler_params=LIMIT,
        cost_estimate=SMALL,
    )(after, own)


def rows_to_send(place, received, mine):
    def kernel(place_ref, received_ref, mine_ref, up_ref, down_ref, sems):
        def send(chosen, to_ref, n, act):
            for ref, use in ((received_ref, chosen), (mine_ref, jnp.logical_not(chosen))):
                pl.when(use)(lambda ref=ref: act(pltpu.make_async_copy(ref, to_ref, sems.at[n])))

        passed_down, passed_up = place_ref[0] == 0, place_ref[0] != RING - 1
        for act in (lambda copy: copy.start(), lambda copy: copy.wait()):
            send(passed_down, down_ref, 0, act)
            send(passed_up, up_ref, 1, act)

    return pl.pallas_call(
        kernel,
        out_shape=[jax.ShapeDtypeStruct(mine.shape, mine.dtype)] * 2,
        in_specs=[SMEM, ANY, ANY],
        out_specs=[HBM, HBM],
        scratch_shapes=[pltpu.SemaphoreType.DMA((2,))],
        compiler_params=LIMIT,
        cost_estimate=SMALL,
    )(place, received, mine)


def columns(group, half):
    e, first = half // PARTS, 0
    for k, part in group:
        count = 2 * half if part is None else 2 * e
        yield k, count, first, [0] if part is None else [part * e, half + part * e]
        first += count


def width(group, half):
    return sum(count for _, count, _, _ in columns(group, half))


def spans(refs, count, e, run):
    if len(refs) > 1 or count == 2 * e:
        run(0, count, lambda: whole(refs))
        return

    @pl.loop(0, count // (2 * e))
    def _(index):
        at = pl.multiple_of(index * 2 * e, 2 * e)
        run(at, 2 * e, lambda: refs[0][pl.ds(at, 2 * e), :])


def whole(refs):
    return refs[0][...] if len(refs) == 1 else jnp.concatenate([ref[...] for ref in refs], axis=0)


def deal(refs, partners):
    refs = iter(refs)
    return [[next(refs) for _ in arrays] for arrays in partners]


def handed_products(handed, partners, group, before=None, room=None, offset=0):
    half, many = handed.shape[0], sum(map(len, partners))
    room = room or width(group, half)

    def kernel(handed_ref, *refs):
        made_ref = refs[-1]
        for (_, count, first, _), tile_refs in zip(columns(group, half), deal(refs, partners)):
            def span(column, columns, partner):
                def strip(at):
                    across = pl.ds(offset + first + column, columns)
                    made_ref[at, across] = product(handed_ref[at, :], partner())
                strips(half, strip)

            spans(tile_refs, count, half // PARTS, span)

    return pl.pallas_call(
        kernel,
        out_shape=jax.ShapeDtypeStruct((half, room), jnp.float32),
        in_specs=[VMEM] * (1 + many) + [VMEM] * (before is not None),
        out_specs=VMEM,
        input_output_aliases={} if before is None else {1 + many: 0},
        compiler_params=LIMIT,
        cost_estimate=SMALL,
    )(handed, *sum(partners, []), *([] if before is None else [before]))


def kept_products(out, weights, kept, theirs, partners, groups, offset=0):
    half, first_call = kept.shape[0], out is None
    many = sum(map(len, partners))

    def kernel(weights_ref, kept_ref, *refs):
        theirs_refs, refs = refs[:len(groups)], refs[len(groups):]
        partner_refs, refs = iter(deal(refs, partners)), refs[many:]
        out_ref, *made_refs, sems = refs if first_call else refs[1:]
        copies = []
        for group, theirs_ref, made_ref in zip(groups, theirs_refs, made_refs):
            for (k, count, first, runs), tile_refs in zip(columns(group, half), partner_refs):
                def span(column, columns, partner):
                    def strip(at):
                        across = pl.ds(first + column, columns)
                        there = pl.ds(offset + first + column, columns)
                        total = product(kept_ref[at, :], partner()) + theirs_ref[at, there]
                        made_ref[at, across] = total * weights_ref[k]
                    strips(half, strip)

                spans(tile_refs, count, half // PARTS, span)
                for n, column in enumerate(runs):
                    run = count // len(runs)
                    copies.append(pltpu.make_async_copy(
                        made_ref.at[:, pl.ds(first + n * run, run)],
                        out_ref.at[k, :, pl.ds(column, run)],
                        sems.at[len(copies)],
                    ))
                    copies[-1].start()
        for copy in copies:
            copy.wait()

    inputs = len(groups) + many
    return pl.pallas_call(
        kernel,
        out_shape=jax.ShapeDtypeStruct((5, half, 2 * half), jnp.float32),
        in_specs=[SMEM] + [VMEM] * (1 + inputs) + [ANY] * (not first_call),
        out_specs=ANY,
        scratch_shapes=[pltpu.VMEM((half, width(group, half)), jnp.float32) for group in groups]
        + [pltpu.SemaphoreType.DMA((2 * sum(map(len, groups)),))],
        input_output_aliases={} if first_call else {2 + inputs: 0},
        compiler_params=LIMIT,
        cost_estimate=SMALL,
    )(weights, kept, *theirs, *sum(partners, []), *([] if first_call else [out]))


def relayed_products(where, rows, partners, blocks, theirs=()):
    e, sums = rows[0][0].shape[0], len(theirs) > 0
    used = sorted({j for parts, *_ in blocks for j in parts})
    sizes = {}
    for parts, _, *places in blocks:
        array, first, *starts = places[sums]
        height, size = sizes.get(array, (0, 0))
        sizes[array] = max(height, first + len(parts) * e), max(size, *(c + e for c in starts))

    def kernel(where_ref, *refs):
        row_refs, refs = deal(refs, rows), refs[2 * len(rows):]
        partner_refs, refs = deal(refs, partners), refs[2 * len(partners):]
        theirs_refs, (*made_refs, taken_ref) = refs[:len(theirs)], refs[len(theirs):]

        def take(kept):
            for n, j in enumerate(used):
                taken_ref[pl.ds(n * e, e), :] = row_refs[j][kept][...]

        for core in range(2):
            pl.when(where_ref[0] == core)(lambda core=core: take(core if sums else 1 - core))

        for parts, partner, *places in blocks:
            taken = taken_ref[pl.ds(used.index(parts[0]) * e, len(parts) * e), :]
            made = product(taken, whole(partner_refs[partner]))
            for n in range(2):
                piece = made[:, n * e:(n + 1) * e]
                if sums:
                    array, first, *starts = places[0]
                    piece += theirs_refs[array][pl.ds(first, len(parts) * e), pl.ds(starts[n], e)]
                array, first, *starts = places[sums]
                made_refs[array][pl.ds(first, len(parts) * e), pl.ds(starts[n], e)] = piece

    operands = sum([*rows, *partners], []) + list(theirs)
    return pl.pallas_call(
        kernel,
        out_shape=[jax.ShapeDtypeStruct(sizes[n], jnp.float32) for n in sorted(sizes)],
        in_specs=[SMEM] + [VMEM] * len(operands),
        out_specs=[VMEM] * len(sizes),
        scratch_shapes=[pltpu.VMEM((len(used) * e, rows[0][0].shape[1]), rows[0][0].dtype)],
        compiler_params=LIMIT,
        cost_estimate=SMALL,
    )(where, *operands)


def scaled_write(out, weights, made, k, regions):
    def kernel(weights_ref, summed_ref, _, out_ref, made_ref, sems):
        copies = []
        for n, (row, column, height, size, to_row, to_column) in enumerate(regions):
            at = pl.ds(row, height), pl.ds(column, size)
            made_ref[at] = summed_ref[at] * weights_ref[k]
            copies.append(pltpu.make_async_copy(
                made_ref.at[at],
                out_ref.at[k, pl.ds(to_row, height), pl.ds(to_column, size)],
                sems.at[n],
            ))
            copies[-1].start()
        for copy in copies:
            copy.wait()

    return pl.pallas_call(
        kernel,
        out_shape=jax.ShapeDtypeStruct(out.shape, jnp.float32),
        in_specs=[SMEM, VMEM, ANY],
        out_specs=ANY,
        scratch_shapes=[
            pltpu.VMEM(made.shape, jnp.float32), pltpu.SemaphoreType.DMA((len(regions),))
        ],
        input_output_aliases={2: 0},
        compiler_params=LIMIT,
        cost_estimate=SMALL,
    )(weights, made, out)


def body(basis_rows, screen):
    blocks = lax.axis_size("blk")
    half = basis_rows.shape[0] // 2
    e = half // PARTS
    column = lax.axis_index("blk") % RING
    core = lax.axis_index("col")
    weights = jnp.concatenate([jnp.ones((1,), jnp.float32), screen[0].astype(jnp.float32)])

    def below(distance):
        return [(i, (i - distance) % blocks) for i in range(blocks)]

    def around(distance):
        return [(i, i - i % RING + (i + distance) % RING) for i in range(blocks)]

    def swap(array):
        return lax.ppermute(array, "col", [(0, 1), (1, 0)])

    place = column.astype(jnp.int32)[None]
    s = dict(where=core.astype(jnp.int32)[None], place=place, held={}, made={}, out=None)

    def fence(*arrived):
        s["held"].update(arrived)
        s.update(lax.optimization_barrier(s))

    def mine(p):
        first = p % 2 * half + p // 2 * e
        s["held"][0, p] = take_rows(s["where"], basis_rows, first, e)

    def fetch4(p):
        return (4, p), lax.ppermute(s["held"][0, p], "blk", below(4))

    def fetch13(p):
        up, down = rows_to_send(s["place"], s["held"][4, p], s["held"][0, p])
        u.append(((3, p), lax.ppermute(up, "blk", around(1))))
        d.append(((1, p), lax.ppermute(down, "blk", around(-1))))

    def part(k, j):
        if j is None:
            return [basis_rows]
        return [s["relayed"]] if k == 2 else [s["held"][k, 2 * j], s["held"][k, 2 * j + 1]]

    def partners(*groups):
        return [part(k, j) for group in groups for k, j in group]

    def make(group, *others, into=None, room=None, offset=0):
        for other in others:
            make(other)
        into = into or group
        s["made"][into] = handed_products(
            s["handed"], partners(group), group, s["made"].get(into), room, offset
        )

    def finish(theirs, *groups, offset=0):
        s["out"] = kept_products(
            s["out"], weights, s["kept"], theirs, partners(*groups), groups, offset
        )

    own, ones = ((0, None),), ((4, 0), (4, 1), (1, 0), (3, 0))
    twos, threes = ((4, 2), (1, 1), (3, 1)), ((4, 3), (1, 2), (3, 2))
    everything = own + ones + twos + threes
    room = width(everything, half)
    places = [sum(width(group, half) for group in (own, ones, twos, threes)[:n]) for n in range(4)]

    s["held"][0, 0] = basis_rows[:e]
    fence()
    mine(1)
    s["kept"] = lax.dynamic_slice_in_dim(basis_rows, core * half, half, 0)
    s["handed"] = lax.dynamic_slice_in_dim(basis_rows, (1 - core) * half, half, 0)
    pieces = 2 * PARTS
    x = [fetch4(0), fetch4(1)]
    fence(x[0])
    d, u = [], []
    fetch13(0)
    for p in range(pieces - 1):
        if p + 2 < pieces:
            mine(p + 2)
            x.append(fetch4(p + 2))
        if p == 1:
            make(own, into=everything, room=room, offset=places[0])
        if p == 3:
            make(ones, into=everything, room=room, offset=places[1])
        if p == 5:
            make(twos, into=everything, room=room, offset=places[2])
        fence(x[p + 1])
        fetch13(p + 1)
        fence(u[p])
        fence(d[p])

    make(threes, into=everything, room=room, offset=places[3])
    some = (0, 1, 2)
    early = [(some, n, (n, 0, 0, e), (0, 0, n * e, (2 + n) * e)) for n in range(2)]
    late = [((3,), n, (0, 0, n * e, (3 + n) * e), (0, 0, n * e, (3 + n) * e)) for n in range(3)]
    late += [((j,), 2, (1, 0, 2 * j * e, (2 * j + 1) * e), (0, e, 2 * j * e, (2 * j + 1) * e)) for j in some]

    def ahead(blocks, *meanwhile):
        rows = [part(1, j) for j in range(1 + max(max(parts) for parts, *_ in blocks))]
        others = [part(3, j) for j in range(1 + max(n for _, n, *_ in blocks))]
        theirs = [swap(array) for array in relayed_products(s["where"], rows, others, blocks)]
        if meanwhile:
            make(*meanwhile)
            fresh = {group: s["made"][group] for group in meanwhile}
            theirs, fresh = lax.optimization_barrier((theirs, fresh))
            s["made"].update(fresh)
        return relayed_products(s["where"], rows, others, blocks, theirs)[0]

    s["ahead"] = ahead(early)
    fence(u[-1])
    fence(d[-1])

    first_sums = lax.ppermute(s["ahead"], "blk", below(-1))
    relayed = lax.ppermute(jnp.concatenate(part(1, 3)), "blk", below(1))
    third, fourth, fifth = ((1, 3),), ((3, 3),), ((2, 3),)
    last_sums = lax.ppermute(ahead(late, third, fourth), "blk", below(-1))
    theirs = [swap(s["made"].pop(everything))]
    finish(theirs, own + ones)
    finish(theirs, twos + threes, offset=places[2])
    s["sums"], s["relayed"] = first_sums, relayed
    fence()

    make(fifth)
    regions = [(0, n * 2 * e, 3 * e, 2 * e, 0, n * half) for n in range(2)]
    s["out"] = scaled_write(s["out"], weights, s["sums"], 2, regions)
    theirs = [swap(s["made"].pop(group)) for group in (third, fourth, fifth)]
    finish(theirs, third, fourth, fifth)
    regions = [(0, n * 3 * e, e, 3 * e, 3 * e, n * half) for n in range(2)]
    regions += [(e, (2 * j + n) * e, e, e, j * e, n * half + 2 * e) for j in some for n in range(2)]
    out = scaled_write(s["out"], weights, last_sums, 2, regions)
    return out[None]


def solution(mesh):
    return jax.shard_map(
        body,
        mesh=mesh,
        in_specs=(P("blk", "col"), P("blk", None)),
        out_specs=P("blk", None, "col", None),
        check_vma=False,
    )
```
